512 devices in a mesh: slab: 64 (over z, y_hi, core), vec: 8 (over y_lo, x).
Axes of the slice: x: 4, y: 4 (y_hi: 2, y_lo: 2; y = y_hi * 2 + y_lo), z: 16, core: 2. Of those that a mesh axis runs over, the one named last changes fastest.
Arguments:
- vectors: bfloat16 [6, 384, 64, 512], P(None, 'vec', 'slab'), may hold values from -0.3125 to 0.3125
- links: bfloat16 [3, 18, 64, 512], P(None, None, 'slab'), may hold values from -2.5 to 2.5
- momenta: int32 [4, 3], replicated, may hold values from -2 to 2
- directions: int32 [3], replicated, may hold values from 0 to 2, each once
- panel_index: int32 [64], replicated, may hold values from 0 to 383, as said below
Outputs:
- elementals: float32 [64, 2, 3, 4, 384], P('slab', None, None, None, 'vec')
The draws below stay inside these ranges and needn't reach their ends.
Inputs may be any that keep to these rules, and one draw needn't show every extreme that they name: `panel_index`: 64 distinct eigenvector numbers; 0 and 383 are among them.
All inputs are finite; a program needn't handle non-finite values.
Results may differ from the reference program's by a relative error of at most 0.004.
Values may be sent and summed in bfloat16 or wider, within the bound.
No kernel may reach another device: no remote copies, remote signals or barrier semaphores. Data moves between devices by JAX's collectives and lax.ppermute only.
A program may use at most 64 MiB of HBM per device.

```python
import math
import jax
import jax.numpy as jnp
from jax import lax

LX = 32
LY = 16
NVEC = 384
PANEL = 64
NMOM = 4
LZ = 64


def draw_panel_index(key, part):
    key = jax.random.fold_in(key, 7)
    inner = jax.random.permutation(key, NVEC - 2)[:PANEL - 2].astype(jnp.int32) + 1
    ends = jnp.array([0, NVEC - 1], dtype=jnp.int32)
    allids = jnp.concatenate([ends, inner])
    order = jax.random.permutation(jax.random.fold_in(key, 1), PANEL)
    return allids[order]


def set_ends(entries, stream_key, low, top_value):
    longest = entries.shape.index(max(entries.shape))
    spots = []
    for shift in (0, 1):
        where = [jax.random.randint(jax.random.fold_in(stream_key, axis), (), 0, length) for axis, length in enumerate(entries.shape)]
        where[longest] = (where[longest] + shift) % entries.shape[longest]
        spots.append(tuple(where))
    return entries.at[spots[0]].set(low).at[spots[1]].set(top_value)


def levels(stream_key, dims, pieces, low, high):
    def one(position, parts):
        steps = jax.random.uniform(jax.random.fold_in(jax.random.fold_in(stream_key, 6), position), (parts,), jnp.float32, low / len(pieces), high / len(pieces))
        return jnp.repeat(jnp.exp(steps), dims[position] // parts).reshape((-1,) + (1,) * (len(dims) - position - 1))

    factor_of = one(*pieces[0])
    for cut in pieces[1:]:
        factor_of = factor_of * one(*cut)
    return factor_of


def normal_values(stream_key, shape, spread, most, pieces=(), held_as=jnp.bfloat16):
    gain = levels(stream_key, shape, pieces, -0.22, 0.18) if pieces else 1.0
    values = jax.random.normal(stream_key, shape, jnp.float32) * spread * gain
    return jnp.minimum(jnp.maximum(values, -most), most).astype(held_as)


def setup_inputs(seed: int = 0) -> dict:
    seeds = jax.random.split(jax.random.key(seed), 6)
    return {
        "vectors": normal_values(seeds[0], (6, NVEC, LZ, LX * LY), ((3 * LX * LY * LZ) ** -0.25), 0.3125, ((1, 8), (2, 64))),
        "links": normal_values(seeds[1], (3, 18, LZ, LX * LY), 0.4, 2.5, ((2, 64),)),
        "momenta": set_ends(jax.random.randint(seeds[2], (NMOM, 3), -2, 3), jax.random.fold_in(seeds[2], 1), -2, 2).astype(jnp.int32),
        "directions": jax.random.permutation(seeds[3], 3).astype(jnp.int32),
        "panel_index": draw_panel_index(jax.random.fold_in(seeds[5], 71), 0),
    }


def roll_sites(values, axis_id, offset):
    shaped = values.reshape(values.shape[:-1] + (LY, LX))
    rolled = jnp.roll(shaped, offset, axis=-1 - axis_id)
    return rolled.reshape(values.shape)


def times_link(link_rows, vector, dagger):
    real_rows = []
    imag_rows = []
    for row_index in range(3):
        total_real = 0.0
        total_imag = 0.0
        for second in range(3):
            if dagger:
                entry_at = second * 3 + row_index
                link_real = link_rows[entry_at][None]
                link_imag = -link_rows[9 + entry_at][None]
            else:
                entry_at = row_index * 3 + second
                link_real = link_rows[entry_at][None]
                link_imag = link_rows[9 + entry_at][None]
            vec_real = vector[second]
            vec_imag = vector[3 + second]
            total_real = total_real + link_real * vec_real - link_imag * vec_imag
            total_imag = total_imag + link_real * vec_imag + link_imag * vec_real
        real_rows.append(total_real)
        imag_rows.append(total_imag)
    return jnp.stack(real_rows + imag_rows)


def site_phase(momenta, z_coord, extent_z):
    x_coord = jnp.arange(LX, dtype=jnp.int32)
    y_coord = jnp.arange(LY, dtype=jnp.int32)
    modulus = LX * LY * extent_z
    numerator = (momenta[:, 0, None, None, None] * x_coord[None, None, None, :] * (LY * extent_z)
                 + momenta[:, 1, None, None, None] * y_coord[None, None, :, None] * (LX * extent_z)
                 + momenta[:, 2, None, None, None] * z_coord[None, :, None, None] * (LX * LY)) % modulus
    angles = numerator.astype(jnp.float32) * (2.0 * math.pi / modulus)
    shape_out = (momenta.shape[0], z_coord.shape[0] * LY * LX)
    return jnp.cos(angles).reshape(shape_out), jnp.sin(angles).reshape(shape_out)


def weigh(panel_vals, cos_part, sin_part):
    cos_b = cos_part[:, None, None, :]
    sin_b = sin_part[:, None, None, :]
    real_part = panel_vals[None, :3] * cos_b - panel_vals[None, 3:] * sin_b
    imag_part = -(panel_vals[None, :3] * sin_b + panel_vals[None, 3:] * cos_b)
    return jnp.stack([real_part, imag_part], 1).astype(jnp.bfloat16)


def pick_directions(directions, shifted):
    onehot = (directions[:, None] == jnp.arange(3, dtype=jnp.int32)[None, :]).astype(jnp.float32)
    chosen = 0.0
    for axis_id in range(3):
        factor = onehot[:, axis_id].reshape((-1,) + (1,) * shifted[axis_id].ndim)
        chosen = chosen + factor * shifted[axis_id][None]
    return chosen


def in_plane(centre, link_f):
    shifted = []
    for axis_id in range(2):
        link_axis = link_f[axis_id]
        forward_term = times_link(link_axis, roll_sites(centre, axis_id, -1), False)
        backward_term = times_link(roll_sites(link_axis, axis_id, 1), roll_sites(centre, axis_id, 1), True)
        shifted.append(0.5 * (forward_term - backward_term))
    return shifted


def reference(vectors, links, momenta, directions, panel_index):
    extent_z = vectors.shape[2]
    nvec = vectors.shape[1]
    npanel = panel_index.shape[0]
    nmom = momenta.shape[0]
    ndir = directions.shape[0]
    panel = jnp.take(vectors, panel_index, axis=1)

    def plane(running, plane_at):
        above_at = (plane_at + 1) % extent_z
        below_at = (plane_at + extent_z - 1) % extent_z
        centre = lax.dynamic_index_in_dim(vectors, plane_at, 2, keepdims=False).astype(jnp.float32)
        forward_field = lax.dynamic_index_in_dim(vectors, above_at, 2, keepdims=False).astype(jnp.float32)
        behind_field = lax.dynamic_index_in_dim(vectors, below_at, 2, keepdims=False).astype(jnp.float32)
        link_f = lax.dynamic_index_in_dim(links, plane_at, 2, keepdims=False).astype(jnp.float32)
        link_below = lax.dynamic_index_in_dim(links, below_at, 2, keepdims=False).astype(jnp.float32)
        shifted = in_plane(centre, link_f)
        shifted.append(0.5 * (times_link(link_f[2], forward_field, False) - times_link(link_below[2], behind_field, True)))
        displaced = pick_directions(directions, shifted).astype(jnp.bfloat16)
        displaced = displaced.reshape(ndir, 2, 3, nvec, LX * LY)
        panel_vals = lax.dynamic_index_in_dim(panel, plane_at, 2, keepdims=False).astype(jnp.float32)
        cos_part, sin_part = site_phase(momenta, plane_at.reshape(1), extent_z)
        weighted = weigh(panel_vals, cos_part, sin_part)
        products = jnp.einsum('mrcps,dtcns->mrpdtn', weighted.astype(jnp.float32), displaced.astype(jnp.float32),
                              precision=lax.Precision.HIGHEST)
        return running + products, None

    start = jnp.zeros((nmom, 2, npanel, ndir, 2, nvec), jnp.float32)
    running, _ = lax.scan(plane, start, jnp.arange(extent_z, dtype=jnp.int32))
    real_part = running[:, 0, :, :, 0] - running[:, 1, :, :, 1]
    imag_part = running[:, 0, :, :, 1] + running[:, 1, :, :, 0]
    return jnp.stack([real_part, imag_part], 0).transpose(2, 0, 3, 1, 4)
```

```python
import functools
import math

import jax
import jax.numpy as jnp
from jax import lax
from jax.experimental import pallas as pl
from jax.experimental.pallas import tpu as pltpu
from jax.sharding import PartitionSpec as P

LX = 32
LY = 16
CAP = 16
TILE = 16
LANES = 128
F32 = jnp.float32
BF16 = jnp.bfloat16
NT = (((1,), (1,)), ((), ()))


def iota(shape, dim):
    return lax.broadcasted_iota(jnp.int32, shape, dim)


def as_column(row):
    n = row.shape[1]
    return jnp.sum(jnp.where(iota((n, n), 0) == iota((n, n), 1), row, 0.0), axis=1, keepdims=True)


def select_kernel(cap, ids_ref, vec_ref, links_ref, pay_ref, up_ref):
    rows, held, sites = vec_ref.shape
    ids = ids_ref[...]
    npanel = ids.shape[1]
    local = ids - lax.axis_index("vec") * held
    inside = (local >= 0) & (local < held)
    mine = jnp.where(inside, 1.0, 0.0)
    before = iota((npanel, npanel), 0) < iota((npanel, npanel), 1)
    rank = jnp.sum(jnp.where(before, as_column(mine), 0.0), axis=0, keepdims=True)
    place = jnp.where(inside, rank, -1.0)
    to_slot = jnp.where(iota((cap, npanel), 0).astype(F32) == place, 1.0, 0.0)
    of_held = jnp.where(iota((held, npanel), 0) == local, 1.0, 0.0)
    pick = lax.dot_general(to_slot, of_held, NT, preferred_element_type=F32).astype(BF16)
    for row in range(rows):
        part = jnp.dot(pick, vec_ref[row], preferred_element_type=F32).astype(BF16)
        for peer in range(pay_ref.shape[0]):
            pay_ref[peer, row * cap:(row + 1) * cap, :] = part
    for row in range(rows):
        up_ref[row * held:(row + 1) * held, :] = vec_ref[row]
    zlink = links_ref[2].astype(F32)
    spare = up_ref.shape[0] - rows * held - zlink.shape[0]
    up_ref[rows * held:, :] = jnp.concatenate([zlink, jnp.zeros((spare, sites), F32)], axis=0).astype(BF16)


def link_terms(ahead, behind, fore, back):
    real, imag = [], []
    for row in range(3):
        re, im = 0.0, 0.0
        for col in range(3):
            ur, ui = fore(row * 3 + col), fore(9 + row * 3 + col)
            re = re + ur * ahead[col] - ui * ahead[3 + col]
            im = im + ur * ahead[3 + col] + ui * ahead[col]
        for col in range(3):
            ur, ui = back(col * 3 + row), back(9 + col * 3 + row)
            re = re - ur * behind[col] - ui * behind[3 + col]
            im = im - ur * behind[3 + col] + ui * behind[col]
        real.append(re)
        imag.append(im)
    return real + imag


def turn_x(value, ahead):
    inner = iota((value.shape[0], LANES), 1) % LX
    parts = []
    for at in range(0, value.shape[1], LANES):
        part = value[:, at:at + LANES]
        if ahead:
            part = jnp.where(inner == LX - 1, pltpu.roll(part, LX - 1, 1), pltpu.roll(part, LANES - 1, 1))
        else:
            part = jnp.where(inner == 0, pltpu.roll(part, LANES - LX + 1, 1), pltpu.roll(part, 1, 1))
        parts.append(part)
    return jnp.concatenate(parts, axis=1)


def turn_y(value, ahead):
    sites = value.shape[1]
    return pltpu.roll(value, sites - LX if ahead else LX, 1)


def planar_kernel(vec_ref, links_ref, out_ref, link_ref, turned_ref):
    rows, held, sites = vec_ref.shape
    for axis_id, turn in enumerate((turn_x, turn_y)):
        link = links_ref[axis_id].astype(F32) * 0.5
        link_ref[2 * axis_id] = link
        link_ref[2 * axis_id + 1] = turn(link, False)

    def step(at, carry):
        first = pl.multiple_of(at * TILE, TILE)
        for row in range(rows):
            value = vec_ref[row, pl.ds(first, TILE), :].astype(F32)
            for axis_id, turn in enumerate((turn_x, turn_y)):
                turned_ref[axis_id, 0, row] = turn(value, True)
                turned_ref[axis_id, 1, row] = turn(value, False)
        for axis_id in range(2):
            for lane in range(0, sites, LANES):
                span = slice(lane, lane + LANES)
                ahead = [turned_ref[axis_id, 0, row, :, span] for row in range(rows)]
                behind = [turned_ref[axis_id, 1, row, :, span] for row in range(rows)]
                shifted = link_terms(
                    ahead, behind,
                    lambda e: link_ref[2 * axis_id, e:e + 1, span],
                    lambda e: link_ref[2 * axis_id + 1, e:e + 1, span],
                )
                for row in range(rows):
                    out_ref[axis_id, pl.ds(first, TILE), row * sites + lane:row * sites + lane + LANES] = (
                        shifted[row].astype(BF16))
        return carry

    lax.fori_loop(0, held // TILE, step, 0)


def main_kernel(cap, momenta_ref, ids_ref, planar_ref, ahead_ref, behind_ref, links_ref, got_ref,
                keep_ref, send_ref, link_ref, field_ref, panel_ref, phase_ref, weight_ref):
    owners = got_ref.shape[0]
    npanel = ids_ref.shape[1]
    held = planar_ref.shape[1]
    sites = got_ref.shape[2]
    rows = got_ref.shape[1] // cap
    nmom = momenta_ref.shape[0]
    slab_id = lax.axis_index("slab")
    core = slab_id % 2

    field_ref[0:2 * held, :] = planar_ref[...].reshape(2 * held, rows * sites)
    link_ref[0] = links_ref[2].astype(F32) * 0.5
    link_ref[1] = behind_ref[rows * held:rows * held + 32, :].astype(F32)[:18] * 0.5

    def z_step(at, carry):
        first = pl.multiple_of(at * TILE, TILE)
        for lane in range(0, sites, LANES):
            span = slice(lane, lane + LANES)
            ahead = [ahead_ref[pl.ds(row * held + first, TILE), span].astype(F32) for row in range(rows)]
            behind = [behind_ref[pl.ds(row * held + first, TILE), span].astype(F32) for row in range(rows)]
            shifted = link_terms(
                ahead, behind,
                lambda e: link_ref[0, e:e + 1, span],
                lambda e: link_ref[1, e:e + 1, span],
            )
            for row in range(rows):
                field_ref[pl.ds(2 * held + first, TILE), row * sites + lane:row * sites + lane + LANES] = (
                    shifted[row].astype(BF16))
        return carry

    lax.fori_loop(0, held // TILE, z_step, 0)

    ids = ids_ref[...]
    owner = jnp.zeros(ids.shape, F32)
    for other in range(1, owners):
        owner = owner + jnp.where(ids >= other * held, 1.0, 0.0)
    owner_col = as_column(owner)
    before = iota((npanel, npanel), 0) < iota((npanel, npanel), 1)
    rank = jnp.sum(jnp.where(before & (owner_col == owner), 1.0, 0.0), axis=0, keepdims=True)
    slot = owner * cap + rank
    place = iota((npanel, npanel), 0)
    half = npanel // 2
    wanted = jnp.where(place < half, 2 * place + core, 2 * (place - half) + 1 - core)
    slot_col = jnp.sum(jnp.where(iota((npanel, npanel), 1) == wanted, slot, 0.0), axis=1, keepdims=True)
    order = jnp.where(iota((npanel, owners * cap), 1).astype(F32) == slot_col, 1.0, 0.0).astype(BF16)
    for row in range(rows):
        block = got_ref[:, row * cap:(row + 1) * cap, :].reshape(owners * cap, sites)
        panel_ref[row] = jnp.dot(order, block, preferred_element_type=F32)

    modulus = sites * lax.axis_size("slab")
    shape = (2 * nmom, sites)
    site, line = iota(shape, 1), iota(shape, 0)
    x_coord, y_coord = site % LX, site // LX
    turns = jnp.zeros(shape, jnp.int32)
    for mom in range(nmom):
        along = (momenta_ref[mom, 0] * (modulus // LX) * x_coord
                 + momenta_ref[mom, 1] * (modulus // LY) * y_coord
                 + momenta_ref[mom, 2] * sites * slab_id)
        turns = jnp.where(line % nmom == mom, along, turns)
    turns = jnp.where(line >= nmom, turns - modulus // 4, turns) & (modulus - 1)
    turns = jnp.where(turns >= modulus // 2, turns - modulus, turns)
    phase_ref[...] = jnp.cos(turns.astype(F32) * (2.0 * math.pi / modulus))

    def weigh(at, carry):
        first = pl.multiple_of(at * TILE, TILE)
        for colour in range(3):
            re = panel_ref[colour, pl.ds(first, TILE), :]
            im = panel_ref[3 + colour, pl.ds(first, TILE), :]
            for mom in range(nmom):
                cos = phase_ref[mom:mom + 1, :]
                sin = phase_ref[nmom + mom:nmom + mom + 1, :]
                wr = (re * cos - im * sin).astype(BF16)
                wi = re * sin + im * cos
                low = slice(colour * sites, (colour + 1) * sites)
                high = slice((3 + colour) * sites, (4 + colour) * sites)
                weight_ref[pl.ds(mom * npanel + first, TILE), low] = wr
                weight_ref[pl.ds(mom * npanel + first, TILE), high] = wi.astype(BF16)
                weight_ref[pl.ds((nmom + mom) * npanel + first, TILE), low] = (-wi).astype(BF16)
                weight_ref[pl.ds((nmom + mom) * npanel + first, TILE), high] = wr
        return carry

    lax.fori_loop(0, npanel // TILE, weigh, 0)
    whole = lax.dot_general(weight_ref[...], field_ref[...], NT, preferred_element_type=F32)
    for part in range(2 * nmom):
        block = whole[part * npanel:(part + 1) * npanel]
        keep_ref[:, part, :] = block[:half]
        send_ref[:, part, :] = block[half:]


def sum_kernel(nmom, directions_ref, parts_ref, out_ref):
    total = jnp.sum(parts_ref[...], axis=0)
    held = out_ref.shape[-1]
    for place in range(out_ref.shape[1]):
        chosen = total[:, 0:held]
        for axis_id in (1, 2):
            along = total[:, axis_id * held:(axis_id + 1) * held]
            chosen = jnp.where(directions_ref[place] == axis_id, along, chosen)
        out_ref[0, place] = chosen[:nmom]
        out_ref[1, place] = chosen[nmom:]


def specs(*spaces):
    return [pl.BlockSpec(memory_space=pltpu.SMEM if s == "s" else pltpu.VMEM) for s in spaces]


def run(cap, vectors, links, momenta, directions, panel_index):
    rows, held, planes, sites = vectors.shape
    npanel = panel_index.shape[0]
    nmom = momenta.shape[0]
    nslab, nvec = lax.axis_size("slab"), lax.axis_size("vec")
    vec = vectors.reshape(rows, held, sites)
    link = links.reshape(3, 18, sites)
    ids = panel_index.reshape(1, npanel)
    params = pltpu.CompilerParams(vmem_limit_bytes=40 * 1024 * 1024)
    shape = jax.ShapeDtypeStruct
    vm = pltpu.VMEM
    pay, up = pl.pallas_call(
        functools.partial(select_kernel, cap),
        out_shape=[shape((nvec, rows * cap, sites), BF16), shape((rows * held + 32, sites), BF16)],
        in_specs=specs("v", "v", "v"), out_specs=specs("v", "v"),
        compiler_params=params, name="select",
    )(ids, vec, link)
    upward = [(i, (i + 1) % nslab) for i in range(nslab)]
    downward = [(j, i) for i, j in upward]
    ahead = lax.ppermute(vec.reshape(rows * held, sites), "slab", downward)
    behind = lax.ppermute(up, "slab", upward)
    got = lax.all_to_all(pay, "vec", 0, 0, tiled=True)
    planar = pl.pallas_call(
        planar_kernel,
        out_shape=shape((2, held, rows * sites), BF16),
        in_specs=specs("v", "v"), out_specs=specs("v")[0],
        scratch_shapes=[vm((4, 18, sites), F32), vm((2, 2, rows, TILE, sites), F32)],
        compiler_params=params, name="planar",
    )(vec, link)
    half = npanel // 2
    part = shape((half, 2 * nmom, 3 * held), F32)
    keep, send = pl.pallas_call(
        functools.partial(main_kernel, cap),
        out_shape=[part, part],
        in_specs=specs("s", "v", "v", "v", "v", "v", "v"), out_specs=specs("v", "v"),
        scratch_shapes=[
            vm((2, 18, sites), F32),
            vm((3 * held, rows * sites), BF16),
            vm((rows, npanel, sites), F32),
            vm((2 * nmom, sites), F32),
            vm((2 * nmom * npanel, rows * sites), BF16),
        ],
        compiler_params=params, name="main",
    )(momenta, ids, planar, ahead, behind, link, got)
    pair = lax.ppermute(send, "slab", [(i, i ^ 1) for i in range(nslab)])
    groups = [[2 * k + c for k in range(nslab // 2)] for c in range(2)]
    parts = lax.all_to_all(keep + pair, "slab", 0, 0, axis_index_groups=groups, tiled=True)
    return pl.pallas_call(
        functools.partial(sum_kernel, nmom),
        out_shape=shape((2, 3, nmom, held), F32),
        in_specs=specs("s", "v"), out_specs=specs("v")[0],
        name="total",
    )(directions, parts)[None]


def body(vectors, links, momenta, directions, panel_index):
    held = vectors.shape[1]
    owner = panel_index // held
    counts = jnp.sum((owner[:, None] == jnp.arange(lax.axis_size("vec"))[None, :]).astype(jnp.int32), axis=0)
    args = (vectors, links, momenta, directions, panel_index)
    return lax.cond(jnp.max(counts) <= CAP, functools.partial(run, CAP), functools.partial(run, held), *args)


def solution(mesh):
    placed = (P(None, "vec", "slab", None), P(None, None, "slab", None), P(), P(), P())
    return jax.shard_map(
        body,
        mesh=mesh,
        in_specs=placed,
        out_specs=P("slab", None, None, None, "vec"),
        check_vma=False,
    )
```

```python
import functools
import math

import jax
import jax.numpy as jnp
from jax import lax
from jax.experimental import pallas as pl
from jax.experimental.pallas import tpu as pltpu
from jax.sharding import PartitionSpec as P

LX = 32
LY = 16
CAP = 16
TILE = 16
LANES = 128
F32 = jnp.float32
BF16 = jnp.bfloat16
NT = (((1,), (1,)), ((), ()))


def iota(shape, dim):
    return lax.broadcasted_iota(jnp.int32, shape, dim)


def as_column(row):
    n = row.shape[1]
    return jnp.sum(jnp.where(iota((n, n), 0) == iota((n, n), 1), row, 0.0), axis=1, keepdims=True)


def owner_and_rank(ids, owners, held):
    npanel = ids.shape[1]
    owner = jnp.zeros(ids.shape, F32)
    for other in range(1, owners):
        owner = owner + jnp.where(ids >= other * held, 1.0, 0.0)
    before = iota((npanel, npanel), 0) < iota((npanel, npanel), 1)
    rank = jnp.sum(jnp.where(before & (as_column(owner) == owner), 1.0, 0.0), axis=0, keepdims=True)
    return owner, rank


def order_of(slot, slots):
    npanel = slot.shape[1]
    half = npanel // 2
    core = lax.axis_index("slab") % 2
    place = iota((npanel, npanel), 0)
    wanted = jnp.where(place < half, 2 * place + core, 2 * (place - half) + 1 - core)
    column = jnp.sum(jnp.where(iota((npanel, npanel), 1) == wanted, slot, 0.0), axis=1, keepdims=True)
    return jnp.where(iota((npanel, slots), 1).astype(F32) == column, 1.0, 0.0).astype(BF16)


def select_kernel(cap, ids_ref, vec_ref, links_ref, pay_ref, up_ref, over_ref):
    rows, held, sites = vec_ref.shape
    ids = ids_ref[...]
    npanel = ids.shape[1]
    local = ids - lax.axis_index("vec") * held
    inside = (local >= 0) & (local < held)
    owner, rank = owner_and_rank(ids, pay_ref.shape[0], held)
    over_ref[0] = (jnp.max(rank) >= cap).astype(jnp.int32)
    place = jnp.where(inside, rank, -1.0)
    to_slot = jnp.where(iota((cap, npanel), 0).astype(F32) == place, 1.0, 0.0)
    of_held = jnp.where(iota((held, npanel), 0) == local, 1.0, 0.0)
    pick = lax.dot_general(to_slot, of_held, NT, preferred_element_type=F32).astype(BF16)
    for row in range(rows):
        part = jnp.dot(pick, vec_ref[row], preferred_element_type=F32).astype(BF16)
        for peer in range(pay_ref.shape[0]):
            pay_ref[peer, row * cap:(row + 1) * cap, :] = part
    for row in range(rows):
        up_ref[row * held:(row + 1) * held, :] = vec_ref[row]
    zlink = links_ref[2].astype(F32)
    spare = up_ref.shape[0] - rows * held - zlink.shape[0]
    up_ref[rows * held:, :] = jnp.concatenate([zlink, jnp.zeros((spare, sites), F32)], axis=0).astype(BF16)


def link_terms(ahead, behind, fore, back):
    real, imag = [], []
    for row in range(3):
        re, im = 0.0, 0.0
        for col in range(3):
            ur, ui = fore(row * 3 + col), fore(9 + row * 3 + col)
            re = re + ur * ahead[col] - ui * ahead[3 + col]
            im = im + ur * ahead[3 + col] + ui * ahead[col]
        for col in range(3):
            ur, ui = back(col * 3 + row), back(9 + col * 3 + row)
            re = re - ur * behind[col] - ui * behind[3 + col]
            im = im - ur * behind[3 + col] + ui * behind[col]
        real.append(re)
        imag.append(im)
    return real + imag


def turn_x(value, ahead):
    inner = iota((value.shape[0], LANES), 1) % LX
    parts = []
    for at in range(0, value.shape[1], LANES):
        part = value[:, at:at + LANES]
        if ahead:
            part = jnp.where(inner == LX - 1, pltpu.roll(part, LX - 1, 1), pltpu.roll(part, LANES - 1, 1))
        else:
            part = jnp.where(inner == 0, pltpu.roll(part, LANES - LX + 1, 1), pltpu.roll(part, 1, 1))
        parts.append(part)
    return jnp.concatenate(parts, axis=1)


def turn_y(value, ahead):
    sites = value.shape[1]
    return pltpu.roll(value, sites - LX if ahead else LX, 1)


def planar_kernel(cap, owners, momenta_ref, ids_ref, vec_ref, links_ref, out_ref, phase_ref, order_ref,
                  link_ref, turned_ref):
    rows, held, sites = vec_ref.shape
    for axis_id, turn in enumerate((turn_x, turn_y)):
        link = links_ref[axis_id].astype(F32) * 0.5
        link_ref[2 * axis_id] = link
        link_ref[2 * axis_id + 1] = turn(link, False)

    def step(at, carry):
        first = pl.multiple_of(at * TILE, TILE)
        for row in range(rows):
            value = vec_ref[row, pl.ds(first, TILE), :].astype(F32)
            for axis_id, turn in enumerate((turn_x, turn_y)):
                turned_ref[axis_id, 0, row] = turn(value, True)
                turned_ref[axis_id, 1, row] = turn(value, False)
        for axis_id in range(2):
            for lane in range(0, sites, LANES):
                span = slice(lane, lane + LANES)
                ahead = [turned_ref[axis_id, 0, row, :, span] for row in range(rows)]
                behind = [turned_ref[axis_id, 1, row, :, span] for row in range(rows)]
                shifted = link_terms(
                    ahead, behind,
                    lambda e: link_ref[2 * axis_id, e:e + 1, span],
                    lambda e: link_ref[2 * axis_id + 1, e:e + 1, span],
                )
                for row in range(rows):
                    out_ref[axis_id, pl.ds(first, TILE), row * sites + lane:row * sites + lane + LANES] = (
                        shifted[row].astype(BF16))
        return carry

    lax.fori_loop(0, held // TILE, step, 0)
    owner, rank = owner_and_rank(ids_ref[...], owners, held)
    order_ref[...] = order_of(owner * cap + rank, owners * cap)
    nmom = momenta_ref.shape[0]
    slab_id = lax.axis_index("slab")
    modulus = sites * lax.axis_size("slab")
    shape = (2 * nmom, sites)
    site, line = iota(shape, 1), iota(shape, 0)
    x_coord, y_coord = site % LX, site // LX
    turns = jnp.zeros(shape, jnp.int32)
    for mom in range(nmom):
        along = (momenta_ref[mom, 0] * (modulus // LX) * x_coord
                 + momenta_ref[mom, 1] * (modulus // LY) * y_coord
                 + momenta_ref[mom, 2] * sites * slab_id)
        turns = jnp.where(line % nmom == mom, along, turns)
    turns = jnp.where(line >= nmom, turns - modulus // 4, turns) & (modulus - 1)
    turns = jnp.where(turns >= modulus // 2, turns - modulus, turns)
    phase_ref[...] = jnp.cos(turns.astype(F32) * (2.0 * math.pi / modulus))


def height_kernel(links_ref, ahead_ref, behind_ref, out_ref, link_ref):
    held, width = out_ref.shape
    sites = links_ref.shape[2]
    rows = width // sites
    link_ref[0] = links_ref[2].astype(F32) * 0.5
    link_ref[1] = behind_ref[rows * held:rows * held + 32, :].astype(F32)[:18] * 0.5

    def step(at, carry):
        first = pl.multiple_of(at * TILE, TILE)
        for lane in range(0, sites, LANES):
            span = slice(lane, lane + LANES)
            ahead = [ahead_ref[pl.ds(row * held + first, TILE), span].astype(F32) for row in range(rows)]
            behind = [behind_ref[pl.ds(row * held + first, TILE), span].astype(F32) for row in range(rows)]
            shifted = link_terms(
                ahead, behind,
                lambda e: link_ref[0, e:e + 1, span],
                lambda e: link_ref[1, e:e + 1, span],
            )
            for row in range(rows):
                out_ref[pl.ds(first, TILE), row * sites + lane:row * sites + lane + LANES] = (
                    shifted[row].astype(BF16))
        return carry

    lax.fori_loop(0, held // TILE, step, 0)


def reorder_kernel(ids_ref, got_ref, out_ref):
    held = got_ref.shape[1] // out_ref.shape[0]
    owners, _, sites = got_ref.shape
    order = order_of(ids_ref[...].astype(F32), owners * held)
    for row in range(out_ref.shape[0]):
        block = got_ref[:, row * held:(row + 1) * held, :].reshape(owners * held, sites)
        out_ref[row] = jnp.dot(order, block, preferred_element_type=F32).astype(BF16)


def main_kernel(cap, over_ref, planar_ref, height_ref, phase_ref, order_ref, got_ref, spare_ref,
                keep_ref, send_ref, field_ref, panel_ref, weight_ref, copied_ref):
    owners = got_ref.shape[0]
    npanel = order_ref.shape[0]
    held = planar_ref.shape[1]
    sites = got_ref.shape[2]
    rows = got_ref.shape[1] // cap
    nmom = phase_ref.shape[0] // 2
    half = npanel // 2
    field_ref[0:2 * held, :] = planar_ref[...].reshape(2 * held, rows * sites)
    field_ref[2 * held:3 * held, :] = height_ref[...]

    @pl.when(over_ref[0] == 0)
    def _():
        for row in range(rows):
            block = got_ref[:, row * cap:(row + 1) * cap, :].reshape(owners * cap, sites)
            panel_ref[row] = jnp.dot(order_ref[...], block, preferred_element_type=F32)

    @pl.when(over_ref[0] != 0)
    def _():
        pltpu.sync_copy(spare_ref, copied_ref)
        panel_ref[...] = copied_ref[...].astype(F32)

    def weigh(at, carry):
        first = pl.multiple_of(at * TILE, TILE)
        for colour in range(3):
            re = panel_ref[colour, pl.ds(first, TILE), :]
            im = panel_ref[3 + colour, pl.ds(first, TILE), :]
            for mom in range(nmom):
                cos = phase_ref[mom:mom + 1, :]
                sin = phase_ref[nmom + mom:nmom + mom + 1, :]
                wr = (re * cos - im * sin).astype(BF16)
                wi = re * sin + im * cos
                low = slice(colour * sites, (colour + 1) * sites)
                high = slice((3 + colour) * sites, (4 + colour) * sites)
                weight_ref[pl.ds(mom * npanel + first, TILE), low] = wr
                weight_ref[pl.ds(mom * npanel + first, TILE), high] = wi.astype(BF16)
                weight_ref[pl.ds((nmom + mom) * npanel + first, TILE), low] = (-wi).astype(BF16)
                weight_ref[pl.ds((nmom + mom) * npanel + first, TILE), high] = wr
        return carry

    lax.fori_loop(0, npanel // TILE, weigh, 0)
    whole = lax.dot_general(weight_ref[...], field_ref[...], NT, preferred_element_type=F32)
    lines = 2 * nmom + 1
    for at, ref in ((0, keep_ref), (half, send_ref)):
        blocks = [whole[part * npanel + at:part * npanel + at + half] for part in range(2 * nmom)]
        for part, block in enumerate(blocks):
            ref[pl.ds(part, half, stride=lines), :] = block[:, :LANES]
        ref[pl.ds(2 * nmom, half, stride=lines), :] = jnp.concatenate([b[:, LANES:] for b in blocks], axis=1)


def sum_kernel(nmom, directions_ref, parts_ref, out_ref):
    total = jnp.sum(parts_ref[...], axis=0)
    held = out_ref.shape[-1]
    spill = 3 * held - LANES
    lines = 2 * nmom
    first = jnp.concatenate([total[:, k * LANES:(k + 1) * LANES] for k in range(lines)], axis=0)
    last = total[:, lines * LANES:]
    last = jnp.concatenate([last[:, k * spill:(k + 1) * spill] for k in range(lines)], axis=0)
    total = jnp.concatenate([first, last], axis=1)
    for place in range(out_ref.shape[1]):
        chosen = total[:, 0:held]
        for axis_id in (1, 2):
            along = total[:, axis_id * held:(axis_id + 1) * held]
            chosen = jnp.where(directions_ref[place] == axis_id, along, chosen)
        out_ref[0, place] = chosen[:nmom]
        out_ref[1, place] = chosen[nmom:]


def specs(*spaces):
    kinds = {"s": pltpu.SMEM, "v": pltpu.VMEM, "a": pl.ANY}
    return [pl.BlockSpec(memory_space=kinds[space]) for space in spaces]


def call(kernel, out_shape, ins, outs, name, scratch=()):
    return pl.pallas_call(
        kernel, out_shape=out_shape, in_specs=specs(*ins), out_specs=specs(*outs),
        scratch_shapes=list(scratch), name=name,
        compiler_params=pltpu.CompilerParams(vmem_limit_bytes=16 * 1024 * 1024),
    )


def body(vectors, links, momenta, directions, panel_index):
    rows, held, planes, sites = vectors.shape
    npanel = panel_index.shape[0]
    nmom = momenta.shape[0]
    nslab, nvec = lax.axis_size("slab"), lax.axis_size("vec")
    half = npanel // 2
    lines = 2 * nmom + 1
    vec = vectors.reshape(rows, held, sites)
    link = links.reshape(3, 18, sites)
    ids = panel_index.reshape(1, npanel)
    shape = jax.ShapeDtypeStruct
    vm = pltpu.VMEM
    pay, up, over = call(
        functools.partial(select_kernel, CAP),
        [shape((nvec, rows * CAP, sites), BF16), shape((rows * held + 32, sites), BF16), shape((1,), jnp.int32)],
        "vvv", "vvs", "select",
    )(ids, vec, link)
    upward = [(i, (i + 1) % nslab) for i in range(nslab)]
    downward = [(j, i) for i, j in upward]
    ahead = lax.ppermute(vec.reshape(rows * held, sites), "slab", downward)
    behind = lax.ppermute(up, "slab", upward)
    got = lax.all_to_all(pay, "vec", 0, 0, tiled=True)

    def gather_all():
        every = jnp.broadcast_to(vec.reshape(1, rows * held, sites), (nvec, rows * held, sites))
        every = lax.all_to_all(every, "vec", 0, 0, tiled=True)
        return call(reorder_kernel, [shape((rows, npanel, sites), BF16)], "vv", "v", "reorder")(ids, every)[0]

    spare = lax.cond(over[0] != 0, gather_all, lambda: jnp.zeros((rows, npanel, sites), BF16))
    planar, phase, order = call(
        functools.partial(planar_kernel, CAP, nvec),
        [shape((2, held, rows * sites), BF16), shape((2 * nmom, sites), F32), shape((npanel, nvec * CAP), BF16)],
        "svvv", "vvv", "planar",
        [vm((4, 18, sites), F32), vm((2, 2, rows, TILE, sites), F32)],
    )(momenta, ids, vec, link)
    height = call(
        height_kernel, [shape((held, rows * sites), BF16)], "vvv", "v", "height", [vm((2, 18, sites), F32)],
    )(link, ahead, behind)[0]
    part = shape((half * lines, LANES), F32)
    keep, send = call(
        functools.partial(main_kernel, CAP), [part, part], "svvvvva", "vv", "main",
        [
            vm((3 * held, rows * sites), BF16),
            vm((rows, npanel, sites), F32),
            vm((2 * nmom * npanel, rows * sites), BF16),
            vm((rows, npanel, sites), BF16),
        ],
    )(over, planar, height, phase, order, got, spare)
    pair = lax.ppermute(send, "slab", [(i, i ^ 1) for i in range(nslab)])
    groups = [[2 * k + c for k in range(nslab // 2)] for c in range(2)]
    both = (keep + pair).reshape(half, 1, lines * LANES)
    parts = lax.all_to_all(both, "slab", 0, 0, axis_index_groups=groups, tiled=True)
    return call(
        functools.partial(sum_kernel, nmom), [shape((2, 3, nmom, held), F32)], "sv", "v", "total",
    )(directions, parts)[0][None]


def solution(mesh):
    placed = (P(None, "vec", "slab", None), P(None, None, "slab", None), P(), P(), P())
    return jax.shard_map(
        body,
        mesh=mesh,
        in_specs=placed,
        out_specs=P("slab", None, None, None, "vec"),
        check_vma=False,
    )
```

```python
import functools
import math

import jax
import jax.numpy as jnp
from jax import lax
from jax.experimental import pallas as pl
from jax.experimental.pallas import tpu as pltpu
from jax.sharding import PartitionSpec as P

LX = 32
LY = 16
CAP = 16
COST = 50_000_000_000
TILE = 16
LANES = 128
F32 = jnp.float32
BF16 = jnp.bfloat16
NT = (((1,), (1,)), ((), ()))


def iota(shape, dim):
    return lax.broadcasted_iota(jnp.int32, shape, dim)


def as_column(row):
    n = row.shape[1]
    return jnp.sum(jnp.where(iota((n, n), 0) == iota((n, n), 1), row, 0.0), axis=1, keepdims=True)


def owner_and_rank(ids, owners, held):
    npanel = ids.shape[1]
    owner = jnp.zeros(ids.shape, F32)
    for other in range(1, owners):
        owner = owner + jnp.where(ids >= other * held, 1.0, 0.0)
    before = iota((npanel, npanel), 0) < iota((npanel, npanel), 1)
    rank = jnp.sum(jnp.where(before & (as_column(owner) == owner), 1.0, 0.0), axis=0, keepdims=True)
    return owner, rank


def order_of(slot, slots):
    npanel = slot.shape[1]
    half = npanel // 2
    core = lax.axis_index("slab") % 2
    place = iota((npanel, npanel), 0)
    wanted = jnp.where(place < half, 2 * place + core, 2 * (place - half) + 1 - core)
    column = jnp.sum(jnp.where(iota((npanel, npanel), 1) == wanted, slot, 0.0), axis=1, keepdims=True)
    return jnp.where(iota((npanel, slots), 1).astype(F32) == column, 1.0, 0.0).astype(BF16)


def select_kernel(cap, ids_ref, vec_ref, pay_ref, over_ref):
    rows, held, sites = vec_ref.shape
    ids = ids_ref[...]
    npanel = ids.shape[1]
    local = ids - lax.axis_index("vec") * held
    inside = (local >= 0) & (local < held)
    owner, rank = owner_and_rank(ids, pay_ref.shape[0], held)
    over_ref[0] = (jnp.max(rank) >= cap).astype(jnp.int32)
    place = jnp.where(inside, rank, -1.0)
    to_slot = jnp.where(iota((cap, npanel), 0).astype(F32) == place, 1.0, 0.0)
    of_held = jnp.where(iota((held, npanel), 0) == local, 1.0, 0.0)
    pick = lax.dot_general(to_slot, of_held, NT, preferred_element_type=F32).astype(BF16)
    for row in range(rows):
        part = jnp.dot(pick, vec_ref[row], preferred_element_type=F32).astype(BF16)
        for peer in range(pay_ref.shape[0]):
            pay_ref[peer, row * cap:(row + 1) * cap, :] = part


def link_terms(ahead, behind, fore, back):
    real, imag = [], []
    for row in range(3):
        re, im = 0.0, 0.0
        for col in range(3):
            ur, ui = fore(row * 3 + col), fore(9 + row * 3 + col)
            re = re + ur * ahead[col] - ui * ahead[3 + col]
            im = im + ur * ahead[3 + col] + ui * ahead[col]
        for col in range(3):
            ur, ui = back(col * 3 + row), back(9 + col * 3 + row)
            re = re - ur * behind[col] - ui * behind[3 + col]
            im = im - ur * behind[3 + col] + ui * behind[col]
        real.append(re)
        imag.append(im)
    return real + imag


def turn_x(value, ahead):
    inner = iota((value.shape[0], LANES), 1) % LX
    parts = []
    for at in range(0, value.shape[1], LANES):
        part = value[:, at:at + LANES]
        if ahead:
            part = jnp.where(inner == LX - 1, pltpu.roll(part, LX - 1, 1), pltpu.roll(part, LANES - 1, 1))
        else:
            part = jnp.where(inner == 0, pltpu.roll(part, LANES - LX + 1, 1), pltpu.roll(part, 1, 1))
        parts.append(part)
    return jnp.concatenate(parts, axis=1)


def turn_y(value, ahead):
    sites = value.shape[1]
    return pltpu.roll(value, sites - LX if ahead else LX, 1)


def planar_kernel(cap, owners, momenta_ref, ids_ref, vec_ref, links_ref, out_ref, phase_ref, order_ref,
                  link_ref, turned_ref):
    rows, held, sites = vec_ref.shape
    for axis_id, turn in enumerate((turn_x, turn_y)):
        link = links_ref[axis_id].astype(F32) * 0.5
        link_ref[2 * axis_id] = link
        link_ref[2 * axis_id + 1] = turn(link, False)

    def step(at, carry):
        first = pl.multiple_of(at * TILE, TILE)
        for row in range(rows):
            value = vec_ref[row, pl.ds(first, TILE), :].astype(F32)
            for axis_id, turn in enumerate((turn_x, turn_y)):
                turned_ref[axis_id, 0, row] = turn(value, True)
                turned_ref[axis_id, 1, row] = turn(value, False)
        for axis_id in range(2):
            for lane in range(0, sites, LANES):
                span = slice(lane, lane + LANES)
                ahead = [turned_ref[axis_id, 0, row, :, span] for row in range(rows)]
                behind = [turned_ref[axis_id, 1, row, :, span] for row in range(rows)]
                shifted = link_terms(
                    ahead, behind,
                    lambda e: link_ref[2 * axis_id, e:e + 1, span],
                    lambda e: link_ref[2 * axis_id + 1, e:e + 1, span],
                )
                for row in range(rows):
                    out_ref[axis_id, pl.ds(first, TILE), row * sites + lane:row * sites + lane + LANES] = (
                        shifted[row].astype(BF16))
        return carry

    lax.fori_loop(0, held // TILE, step, 0)
    owner, rank = owner_and_rank(ids_ref[...], owners, held)
    fits = jnp.max(rank, axis=1, keepdims=True) < cap
    order_ref[...] = order_of(jnp.where(fits, owner * cap + rank, -1.0), owners * cap)
    nmom = momenta_ref.shape[0]
    slab_id = lax.axis_index("slab")
    modulus = sites * lax.axis_size("slab")
    shape = (2 * nmom, sites)
    site, line = iota(shape, 1), iota(shape, 0)
    x_coord, y_coord = site % LX, site // LX
    turns = jnp.zeros(shape, jnp.int32)
    for mom in range(nmom):
        along = (momenta_ref[mom, 0] * (modulus // LX) * x_coord
                 + momenta_ref[mom, 1] * (modulus // LY) * y_coord
                 + momenta_ref[mom, 2] * sites * slab_id)
        turns = jnp.where(line % nmom == mom, along, turns)
    turns = jnp.where(line >= nmom, turns - modulus // 4, turns) & (modulus - 1)
    turns = jnp.where(turns >= modulus // 2, turns - modulus, turns)
    phase_ref[...] = jnp.cos(turns.astype(F32) * (2.0 * math.pi / modulus))


def height_kernel(links_ref, below_ref, inner_ref, outer_ref, out_ref, link_ref):
    first_core = lax.axis_index("slab") % 2 == 0
    pl.when(first_core)(lambda: height(links_ref, below_ref, inner_ref, outer_ref, out_ref, link_ref))
    pl.when(jnp.logical_not(first_core))(lambda: height(links_ref, below_ref, outer_ref, inner_ref, out_ref, link_ref))


def height(links_ref, below_ref, ahead_ref, behind_ref, out_ref, link_ref):
    held, width = out_ref.shape
    sites = links_ref.shape[2]
    rows = width // sites
    link_ref[0] = links_ref[2].astype(F32) * 0.5
    link_ref[1] = below_ref[2].astype(F32) * 0.5

    def step(at, carry):
        first = pl.multiple_of(at * TILE, TILE)
        for lane in range(0, sites, LANES):
            span = slice(lane, lane + LANES)
            ahead = [ahead_ref[pl.ds(row * held + first, TILE), span].astype(F32) for row in range(rows)]
            behind = [behind_ref[pl.ds(row * held + first, TILE), span].astype(F32) for row in range(rows)]
            shifted = link_terms(
                ahead, behind,
                lambda e: link_ref[0, e:e + 1, span],
                lambda e: link_ref[1, e:e + 1, span],
            )
            for row in range(rows):
                out_ref[pl.ds(first, TILE), row * sites + lane:row * sites + lane + LANES] = (
                    shifted[row].astype(BF16))
        return carry

    lax.fori_loop(0, held // TILE, step, 0)


def reorder_kernel(ids_ref, got_ref, out_ref):
    held = got_ref.shape[1] // out_ref.shape[0]
    owners, _, sites = got_ref.shape
    order = order_of(ids_ref[...].astype(F32), owners * held)
    for row in range(out_ref.shape[0]):
        block = got_ref[:, row * held:(row + 1) * held, :].reshape(owners * held, sites)
        out_ref[row] = jnp.dot(order, block, preferred_element_type=F32).astype(BF16)


def main_kernel(cap, planar_ref, height_ref, phase_ref, order_ref, got_ref, spare_ref,
                keep_ref, send_ref, field_ref, panel_ref, weight_ref):
    owners = got_ref.shape[0]
    npanel = order_ref.shape[0]
    held = planar_ref.shape[1]
    sites = got_ref.shape[2]
    rows = got_ref.shape[1] // cap
    nmom = phase_ref.shape[0] // 2
    half = npanel // 2
    field_ref[0:2 * held, :] = planar_ref[...].reshape(2 * held, rows * sites)
    field_ref[2 * held:3 * held, :] = height_ref[...]
    for row in range(rows):
        block = got_ref[:, row * cap:(row + 1) * cap, :].reshape(owners * cap, sites)
        picked = jnp.dot(order_ref[...], block, preferred_element_type=F32)
        panel_ref[row] = picked + spare_ref[row].astype(F32)

    def weigh(at, carry):
        first = pl.multiple_of(at * TILE, TILE)
        for colour in range(3):
            re = panel_ref[colour, pl.ds(first, TILE), :]
            im = panel_ref[3 + colour, pl.ds(first, TILE), :]
            for mom in range(nmom):
                cos = phase_ref[mom:mom + 1, :]
                sin = phase_ref[nmom + mom:nmom + mom + 1, :]
                wr = (re * cos - im * sin).astype(BF16)
                wi = re * sin + im * cos
                low = slice(colour * sites, (colour + 1) * sites)
                high = slice((3 + colour) * sites, (4 + colour) * sites)
                weight_ref[pl.ds(mom * npanel + first, TILE), low] = wr
                weight_ref[pl.ds(mom * npanel + first, TILE), high] = wi.astype(BF16)
                weight_ref[pl.ds((nmom + mom) * npanel + first, TILE), low] = (-wi).astype(BF16)
                weight_ref[pl.ds((nmom + mom) * npanel + first, TILE), high] = wr
        return carry

    lax.fori_loop(0, npanel // TILE, weigh, 0)
    whole = lax.dot_general(weight_ref[...], field_ref[...], NT, preferred_element_type=F32)
    lines = 2 * nmom + 1
    for at, ref in ((0, keep_ref), (half, send_ref)):
        blocks = [whole[part * npanel + at:part * npanel + at + half] for part in range(2 * nmom)]
        for part, block in enumerate(blocks):
            ref[pl.ds(part, half, stride=lines), :] = block[:, :LANES]
        ref[pl.ds(2 * nmom, half, stride=lines), :] = jnp.concatenate([b[:, LANES:] for b in blocks], axis=1)


def sum_kernel(nmom, directions_ref, parts_ref, out_ref):
    total = jnp.sum(parts_ref[...], axis=0)
    held = out_ref.shape[-1]
    spill = 3 * held - LANES
    lines = 2 * nmom
    first = jnp.concatenate([total[:, k * LANES:(k + 1) * LANES] for k in range(lines)], axis=0)
    last = total[:, lines * LANES:]
    last = jnp.concatenate([last[:, k * spill:(k + 1) * spill] for k in range(lines)], axis=0)
    total = jnp.concatenate([first, last], axis=1)
    for place in range(out_ref.shape[1]):
        chosen = total[:, 0:held]
        for axis_id in (1, 2):
            along = total[:, axis_id * held:(axis_id + 1) * held]
            chosen = jnp.where(directions_ref[:, place:place + 1] == axis_id, along, chosen)
        out_ref[0, place] = chosen[:nmom]
        out_ref[1, place] = chosen[nmom:]


def specs(*spaces):
    kinds = {"s": pltpu.SMEM, "v": pltpu.VMEM, "a": pl.ANY}
    return [pl.BlockSpec(memory_space=kinds[space]) for space in spaces]


def call(kernel, out_shape, ins, outs, name, scratch=(), cost=0):
    return pl.pallas_call(
        kernel, out_shape=out_shape, in_specs=specs(*ins), out_specs=specs(*outs),
        scratch_shapes=list(scratch), name=name,
        cost_estimate=pl.CostEstimate(flops=cost, bytes_accessed=0, transcendentals=0) if cost else None,
        compiler_params=pltpu.CompilerParams(vmem_limit_bytes=16 * 1024 * 1024),
    )


def in_vmem(value):
    return pltpu.with_memory_space_constraint(value, pltpu.VMEM)


def body(vectors, links, momenta, directions, panel_index):
    rows, held, planes, sites = vectors.shape
    npanel = panel_index.shape[0]
    nmom = momenta.shape[0]
    nslab, nvec = lax.axis_size("slab"), lax.axis_size("vec")
    half = npanel // 2
    lines = 2 * nmom + 1
    vec = vectors.reshape(rows, held, sites)
    link = links.reshape(3, 18, sites)
    ids = panel_index.reshape(1, npanel)
    shape = jax.ShapeDtypeStruct
    vm = pltpu.VMEM
    flat = vec.reshape(rows * held, sites)
    mate = [(i, i ^ 1) for i in range(nslab)]
    beyond = [(i, (i + 1) % nslab if i % 2 else (i - 1) % nslab) for i in range(nslab)]
    upward = [(i, (i + 1) % nslab) for i in range(nslab)]
    outer = lax.ppermute(flat, "slab", beyond)
    pay, over = call(
        functools.partial(select_kernel, CAP), [shape((nvec, rows * CAP, sites), BF16), shape((1,), jnp.int32)],
        "vv", "vs", "select", (), COST,
    )(in_vmem(ids), in_vmem(vec))
    got = lax.all_to_all(pay, "vec", 0, 0, tiled=True)
    def gather_all():
        every = jnp.broadcast_to(vec.reshape(1, rows * held, sites), (nvec, rows * held, sites))
        every = lax.all_to_all(every, "vec", 0, 0, tiled=True)
        return call(reorder_kernel, [shape((rows, npanel, sites), BF16)], "vv", "v", "reorder")(ids, every)[0]

    planar, phase, order = call(
        functools.partial(planar_kernel, CAP, nvec),
        [shape((2, held, rows * sites), BF16), shape((2 * nmom, sites), F32), shape((npanel, nvec * CAP), BF16)],
        "svvv", "vvv", "planar",
        [vm((4, 18, sites), F32), vm((2, 2, rows, TILE, sites), F32)], COST,
    )(momenta, ids, vec, link)
    spare = lax.cond(over[0] != 0, gather_all, lambda: jnp.zeros((rows, npanel, sites), BF16))
    outer, flat_late, link_late = lax.optimization_barrier((outer, flat, link))
    inner = lax.ppermute(flat_late, "slab", mate)
    below = lax.ppermute(link_late, "slab", upward)
    height = call(
        height_kernel, [shape((held, rows * sites), BF16)], "vvvv", "v", "height", [vm((2, 18, sites), F32)],
    )(link, below, inner, outer)[0]
    part = shape((half * lines, LANES), F32)
    keep, send = call(
        functools.partial(main_kernel, CAP), [part, part], "vvvvvv", "vv", "main",
        [
            vm((3 * held, rows * sites), BF16),
            vm((rows, npanel, sites), F32),
            vm((2 * nmom * npanel, rows * sites), BF16),
        ],
    )(planar, height, in_vmem(phase), in_vmem(order), got, in_vmem(spare))
    pair = lax.ppermute(send, "slab", mate)
    groups = [[2 * k + c for k in range(nslab // 2)] for c in range(2)]
    both = (keep + pair).reshape(half, 1, lines * LANES)
    parts = lax.all_to_all(both, "slab", 0, 0, axis_index_groups=groups, tiled=True)
    return call(
        functools.partial(sum_kernel, nmom), [shape((2, 3, nmom, held), F32)], "vv", "v", "total",
    )(in_vmem(directions.reshape(1, 3)), parts)[0][None]


def solution(mesh):
    placed = (P(None, "vec", "slab", None), P(None, None, "slab", None), P(), P(), P())
    return jax.shard_map(
        body,
        mesh=mesh,
        in_specs=placed,
        out_specs=P("slab", None, None, None, "vec"),
        check_vma=False,
    )
```

```python
import functools
import math

import jax
import jax.numpy as jnp
from jax import lax
from jax.experimental import pallas as pl
from jax.experimental.pallas import tpu as pltpu
from jax.sharding import PartitionSpec as P

LX = 32
LY = 16
CAP = 16
COST = 50_000_000_000
TILE = 16
LANES = 128
F32 = jnp.float32
BF16 = jnp.bfloat16
NT = (((1,), (1,)), ((), ()))


def iota(shape, dim):
    return lax.broadcasted_iota(jnp.int32, shape, dim)


def as_column(row):
    n = row.shape[1]
    return jnp.sum(jnp.where(iota((n, n), 0) == iota((n, n), 1), row, 0.0), axis=1, keepdims=True)


def owner_and_rank(ids, owners, held):
    npanel = ids.shape[1]
    owner = jnp.zeros(ids.shape, F32)
    for other in range(1, owners):
        owner = owner + jnp.where(ids >= other * held, 1.0, 0.0)
    before = iota((npanel, npanel), 0) < iota((npanel, npanel), 1)
    rank = jnp.sum(jnp.where(before & (as_column(owner) == owner), 1.0, 0.0), axis=0, keepdims=True)
    return owner, rank


def order_of(slot, slots):
    npanel = slot.shape[1]
    half = npanel // 2
    core = lax.axis_index("slab") % 2
    place = iota((npanel, npanel), 0)
    wanted = jnp.where(place < half, 2 * place + core, 2 * (place - half) + 1 - core)
    column = jnp.sum(jnp.where(iota((npanel, npanel), 1) == wanted, slot, 0.0), axis=1, keepdims=True)
    return jnp.where(iota((npanel, slots), 1).astype(F32) == column, 1.0, 0.0).astype(BF16)


def select_kernel(cap, ids_ref, vec_ref, pay_ref, over_ref, here_ref, held_ref, block_ref, in_sem, out_sem):
    ids_load = pltpu.make_async_copy(ids_ref, here_ref, in_sem.at[0])
    load = pltpu.make_async_copy(vec_ref, held_ref, in_sem.at[1])
    ids_load.start()
    load.start()
    rows, held, sites = vec_ref.shape
    ids_load.wait()
    ids = here_ref[...]
    npanel = ids.shape[1]
    local = ids - lax.axis_index("vec") * held
    inside = (local >= 0) & (local < held)
    owner, rank = owner_and_rank(ids, pay_ref.shape[0], held)
    over_ref[0] = (jnp.max(rank) >= cap).astype(jnp.int32)
    place = jnp.where(inside, rank, -1.0)
    to_slot = jnp.where(iota((cap, npanel), 0).astype(F32) == place, 1.0, 0.0)
    of_held = jnp.where(iota((held, npanel), 0) == local, 1.0, 0.0)
    pick = lax.dot_general(to_slot, of_held, NT, preferred_element_type=F32).astype(BF16)
    load.wait()
    for row in range(rows):
        block_ref[row * cap:(row + 1) * cap, :] = jnp.dot(
            pick, held_ref[row], preferred_element_type=F32).astype(BF16)
    copies = [pltpu.make_async_copy(block_ref, pay_ref.at[peer], out_sem.at[peer]) for peer in range(pay_ref.shape[0])]
    for copy in copies:
        copy.start()
    for copy in copies:
        copy.wait()


def link_terms(ahead, behind, fore, back):
    real, imag = [], []
    for row in range(3):
        re, im = 0.0, 0.0
        for col in range(3):
            ur, ui = fore(row * 3 + col), fore(9 + row * 3 + col)
            re = re + ur * ahead[col] - ui * ahead[3 + col]
            im = im + ur * ahead[3 + col] + ui * ahead[col]
        for col in range(3):
            ur, ui = back(col * 3 + row), back(9 + col * 3 + row)
            re = re - ur * behind[col] - ui * behind[3 + col]
            im = im - ur * behind[3 + col] + ui * behind[col]
        real.append(re)
        imag.append(im)
    return real + imag


def turn_x(value, ahead):
    inner = iota((value.shape[0], LANES), 1) % LX
    parts = []
    for at in range(0, value.shape[1], LANES):
        part = value[:, at:at + LANES]
        if ahead:
            part = jnp.where(inner == LX - 1, pltpu.roll(part, LX - 1, 1), pltpu.roll(part, LANES - 1, 1))
        else:
            part = jnp.where(inner == 0, pltpu.roll(part, LANES - LX + 1, 1), pltpu.roll(part, 1, 1))
        parts.append(part)
    return jnp.concatenate(parts, axis=1)


def turn_y(value, ahead):
    sites = value.shape[1]
    return pltpu.roll(value, sites - LX if ahead else LX, 1)


def planar_kernel(cap, owners, momenta_ref, ids_ref, vec_ref, links_ref, out_ref, phase_ref, order_ref,
                  link_ref, turned_ref):
    rows, held, sites = vec_ref.shape
    for axis_id, turn in enumerate((turn_x, turn_y)):
        link = links_ref[axis_id].astype(F32) * 0.5
        link_ref[2 * axis_id] = link
        link_ref[2 * axis_id + 1] = turn(link, False)

    def step(at, carry):
        first = pl.multiple_of(at * TILE, TILE)
        for row in range(rows):
            value = vec_ref[row, pl.ds(first, TILE), :].astype(F32)
            for axis_id, turn in enumerate((turn_x, turn_y)):
                turned_ref[axis_id, 0, row] = turn(value, True)
                turned_ref[axis_id, 1, row] = turn(value, False)
        for axis_id in range(2):
            for lane in range(0, sites, LANES):
                span = slice(lane, lane + LANES)
                ahead = [turned_ref[axis_id, 0, row, :, span] for row in range(rows)]
                behind = [turned_ref[axis_id, 1, row, :, span] for row in range(rows)]
                shifted = link_terms(
                    ahead, behind,
                    lambda e: link_ref[2 * axis_id, e:e + 1, span],
                    lambda e: link_ref[2 * axis_id + 1, e:e + 1, span],
                )
                for row in range(rows):
                    out_ref[axis_id, pl.ds(first, TILE), row * sites + lane:row * sites + lane + LANES] = (
                        shifted[row].astype(BF16))
        return carry

    lax.fori_loop(0, held // TILE, step, 0)
    owner, rank = owner_and_rank(ids_ref[...], owners, held)
    fits = jnp.max(rank, axis=1, keepdims=True) < cap
    order_ref[...] = order_of(jnp.where(fits, owner * cap + rank, -1.0), owners * cap)
    nmom = momenta_ref.shape[0]
    slab_id = lax.axis_index("slab")
    modulus = sites * lax.axis_size("slab")
    shape = (2 * nmom, sites)
    site, line = iota(shape, 1), iota(shape, 0)
    x_coord, y_coord = site % LX, site // LX
    turns = jnp.zeros(shape, jnp.int32)
    for mom in range(nmom):
        along = (momenta_ref[mom, 0] * (modulus // LX) * x_coord
                 + momenta_ref[mom, 1] * (modulus // LY) * y_coord
                 + momenta_ref[mom, 2] * sites * slab_id)
        turns = jnp.where(line % nmom == mom, along, turns)
    turns = jnp.where(line >= nmom, turns - modulus // 4, turns) & (modulus - 1)
    turns = jnp.where(turns >= modulus // 2, turns - modulus, turns)
    phase_ref[...] = jnp.cos(turns.astype(F32) * (2.0 * math.pi / modulus))


def height_kernel(links_ref, below_ref, inner_ref, outer_ref, out_ref, link_ref):
    first_core = lax.axis_index("slab") % 2 == 0
    pl.when(first_core)(lambda: height(links_ref, below_ref, inner_ref, outer_ref, out_ref, link_ref))
    pl.when(jnp.logical_not(first_core))(lambda: height(links_ref, below_ref, outer_ref, inner_ref, out_ref, link_ref))


def height(links_ref, below_ref, ahead_ref, behind_ref, out_ref, link_ref):
    held, width = out_ref.shape
    sites = links_ref.shape[2]
    rows = width // sites
    link_ref[0] = links_ref[2].astype(F32) * 0.5
    link_ref[1] = below_ref[2].astype(F32) * 0.5

    def step(at, carry):
        first = pl.multiple_of(at * TILE, TILE)
        for lane in range(0, sites, LANES):
            span = slice(lane, lane + LANES)
            ahead = [ahead_ref[pl.ds(row * held + first, TILE), span].astype(F32) for row in range(rows)]
            behind = [behind_ref[pl.ds(row * held + first, TILE), span].astype(F32) for row in range(rows)]
            shifted = link_terms(
                ahead, behind,
                lambda e: link_ref[0, e:e + 1, span],
                lambda e: link_ref[1, e:e + 1, span],
            )
            for row in range(rows):
                out_ref[pl.ds(first, TILE), row * sites + lane:row * sites + lane + LANES] = (
                    shifted[row].astype(BF16))
        return carry

    lax.fori_loop(0, held // TILE, step, 0)


def reorder_kernel(ids_ref, got_ref, out_ref):
    held = got_ref.shape[1] // out_ref.shape[0]
    owners, _, sites = got_ref.shape
    order = order_of(ids_ref[...].astype(F32), owners * held)
    for row in range(out_ref.shape[0]):
        block = got_ref[:, row * held:(row + 1) * held, :].reshape(owners * held, sites)
        out_ref[row] = jnp.dot(order, block, preferred_element_type=F32).astype(BF16)


def main_kernel(cap, half_at, planar_ref, height_ref, phase_ref, order_ref, got_ref, spare_ref,
                out_ref, field_ref, panel_ref, weight_ref):
    owners = got_ref.shape[0]
    npanel = order_ref.shape[0] // 2
    held = planar_ref.shape[1]
    sites = got_ref.shape[2]
    rows = got_ref.shape[1] // cap
    nmom = phase_ref.shape[0] // 2
    chosen = slice(half_at * npanel, (half_at + 1) * npanel)
    field_ref[0:2 * held, :] = planar_ref[...].reshape(2 * held, rows * sites)
    field_ref[2 * held:3 * held, :] = height_ref[...]
    for row in range(rows):
        block = got_ref[:, row * cap:(row + 1) * cap, :].reshape(owners * cap, sites)
        picked = jnp.dot(order_ref[chosen, :], block, preferred_element_type=F32)
        panel_ref[row] = picked + spare_ref[row, chosen, :].astype(F32)

    def weigh(at, carry):
        first = pl.multiple_of(at * TILE, TILE)
        for colour in range(3):
            re = panel_ref[colour, pl.ds(first, TILE), :]
            im = panel_ref[3 + colour, pl.ds(first, TILE), :]
            for mom in range(nmom):
                cos = phase_ref[mom:mom + 1, :]
                sin = phase_ref[nmom + mom:nmom + mom + 1, :]
                wr = (re * cos - im * sin).astype(BF16)
                wi = re * sin + im * cos
                low = slice(colour * sites, (colour + 1) * sites)
                high = slice((3 + colour) * sites, (4 + colour) * sites)
                weight_ref[pl.ds(mom * npanel + first, TILE), low] = wr
                weight_ref[pl.ds(mom * npanel + first, TILE), high] = wi.astype(BF16)
                weight_ref[pl.ds((nmom + mom) * npanel + first, TILE), low] = (-wi).astype(BF16)
                weight_ref[pl.ds((nmom + mom) * npanel + first, TILE), high] = wr
        return carry

    lax.fori_loop(0, npanel // TILE, weigh, 0)
    whole = lax.dot_general(weight_ref[...], field_ref[...], NT, preferred_element_type=F32)
    lines = 2 * nmom + 1
    blocks = [whole[part * npanel:(part + 1) * npanel] for part in range(2 * nmom)]
    for part, block in enumerate(blocks):
        out_ref[pl.ds(part, npanel, stride=lines), :] = block[:, :LANES]
    out_ref[pl.ds(2 * nmom, npanel, stride=lines), :] = jnp.concatenate([b[:, LANES:] for b in blocks], axis=1)


def sum_kernel(nmom, directions_ref, parts_ref, out_ref):
    total = jnp.sum(parts_ref[...], axis=0)
    held = out_ref.shape[-1]
    spill = 3 * held - LANES
    lines = 2 * nmom
    first = jnp.concatenate([total[:, k * LANES:(k + 1) * LANES] for k in range(lines)], axis=0)
    last = total[:, lines * LANES:]
    last = jnp.concatenate([last[:, k * spill:(k + 1) * spill] for k in range(lines)], axis=0)
    total = jnp.concatenate([first, last], axis=1)
    for place in range(out_ref.shape[1]):
        chosen = total[:, 0:held]
        for axis_id in (1, 2):
            along = total[:, axis_id * held:(axis_id + 1) * held]
            chosen = jnp.where(directions_ref[:, place:place + 1] == axis_id, along, chosen)
        out_ref[0, place] = chosen[:nmom]
        out_ref[1, place] = chosen[nmom:]


def specs(*spaces):
    kinds = {"s": pltpu.SMEM, "v": pltpu.VMEM, "a": pl.ANY, "h": pltpu.HBM}
    return [pl.BlockSpec(memory_space=kinds[space]) for space in spaces]


def call(kernel, out_shape, ins, outs, name, scratch=(), cost=0):
    return pl.pallas_call(
        kernel, out_shape=out_shape, in_specs=specs(*ins), out_specs=specs(*outs),
        scratch_shapes=list(scratch), name=name,
        cost_estimate=pl.CostEstimate(flops=cost, bytes_accessed=0, transcendentals=0) if cost else None,
        compiler_params=pltpu.CompilerParams(vmem_limit_bytes=16 * 1024 * 1024),
    )


def in_vmem(value):
    return pltpu.with_memory_space_constraint(value, pltpu.VMEM)


def body(vectors, links, momenta, directions, panel_index):
    rows, held, planes, sites = vectors.shape
    npanel = panel_index.shape[0]
    nmom = momenta.shape[0]
    nslab, nvec = lax.axis_size("slab"), lax.axis_size("vec")
    half = npanel // 2
    lines = 2 * nmom + 1
    vec = vectors.reshape(rows, held, sites)
    link = links.reshape(3, 18, sites)
    ids = panel_index.reshape(1, npanel)
    shape = jax.ShapeDtypeStruct
    vm = pltpu.VMEM
    flat = vec.reshape(rows * held, sites)
    mate = [(i, i ^ 1) for i in range(nslab)]
    beyond = [(i, (i + 1) % nslab if i % 2 else (i - 1) % nslab) for i in range(nslab)]
    upward = [(i, (i + 1) % nslab) for i in range(nslab)]
    outer = lax.ppermute(flat, "slab", beyond)
    pay, over = call(
        functools.partial(select_kernel, CAP), [shape((nvec, rows * CAP, sites), BF16), pltpu.SMEM((1,), jnp.int32)],
        "hh", "as", "select",
        [vm(ids.shape, jnp.int32), vm(vec.shape, BF16), vm((rows * CAP, sites), BF16), pltpu.SemaphoreType.DMA((2,)),
         pltpu.SemaphoreType.DMA((nvec,))],
        COST,
    )(ids, vec)
    got = lax.all_to_all(pay, "vec", 0, 0, tiled=True)
    def gather_all():
        every = jnp.broadcast_to(vec.reshape(1, rows * held, sites), (nvec, rows * held, sites))
        every = lax.all_to_all(every, "vec", 0, 0, tiled=True)
        return call(reorder_kernel, [shape((rows, npanel, sites), BF16)], "vv", "v", "reorder")(ids, every)[0]

    planar, phase, order = call(
        functools.partial(planar_kernel, CAP, nvec),
        [shape((2, held, rows * sites), BF16), shape((2 * nmom, sites), F32), shape((npanel, nvec * CAP), BF16)],
        "svvv", "vvv", "planar",
        [vm((4, 18, sites), F32), vm((2, 2, rows, TILE, sites), F32)], COST,
    )(momenta, ids, vec, link)
    spare = lax.cond(over[0] != 0, gather_all, lambda: jnp.zeros((rows, npanel, sites), BF16))
    outer, flat_late, link_late = lax.optimization_barrier((outer, flat, link))
    inner = lax.ppermute(flat_late, "slab", mate)
    below = lax.ppermute(link_late, "slab", upward)
    height = call(
        height_kernel, [shape((held, rows * sites), BF16)], "vvvv", "v", "height", [vm((2, 18, sites), F32)],
    )(link, below, inner, outer)[0]
    part = shape((half * lines, LANES), F32)
    inputs = (planar, height, in_vmem(phase), in_vmem(order), got, in_vmem(spare))
    send, keep = [
        call(
            functools.partial(main_kernel, CAP, half_at), [part], "vvvvvv", "v", name,
            [vm((3 * held, rows * sites), BF16), vm((rows, half, sites), F32),
             vm((2 * nmom * half, rows * sites), BF16)],
            cost,
        )(*inputs)[0]
        for half_at, name, cost in ((1, "send", 0), (0, "keep", COST))
    ]
    pair = lax.ppermute(send, "slab", mate)
    groups = [[2 * k + c for k in range(nslab // 2)] for c in range(2)]
    both = (keep + pair).reshape(half, 1, lines * LANES)
    parts = lax.all_to_all(both, "slab", 0, 0, axis_index_groups=groups, tiled=True)
    return call(
        functools.partial(sum_kernel, nmom), [shape((2, 3, nmom, held), F32)], "vv", "v", "total",
    )(in_vmem(directions.reshape(1, 3)), parts)[0][None]


def solution(mesh):
    placed = (P(None, "vec", "slab", None), P(None, None, "slab", None), P(), P(), P())
    return jax.shard_map(
        body,
        mesh=mesh,
        in_specs=placed,
        out_specs=P("slab", None, None, None, "vec"),
        check_vma=False,
    )
```

```python
import functools
import math

import jax
import jax.numpy as jnp
from jax import lax
from jax.experimental import pallas as pl
from jax.experimental.pallas import tpu as pltpu
from jax.sharding import PartitionSpec as P

LX = 32
LY = 16
CAP = 16
COST = 50_000_000_000
TILE = 16
LANES = 128
F32 = jnp.float32
BF16 = jnp.bfloat16
NT = (((1,), (1,)), ((), ()))


def iota(shape, dim):
    return lax.broadcasted_iota(jnp.int32, shape, dim)


def as_column(row):
    n = row.shape[1]
    return jnp.sum(jnp.where(iota((n, n), 0) == iota((n, n), 1), row, 0.0), axis=1, keepdims=True)


def owner_and_rank(ids, owners, held):
    npanel = ids.shape[1]
    owner = jnp.zeros(ids.shape, F32)
    for other in range(1, owners):
        owner = owner + jnp.where(ids >= other * held, 1.0, 0.0)
    before = iota((npanel, npanel), 0) < iota((npanel, npanel), 1)
    rank = jnp.sum(jnp.where(before & (as_column(owner) == owner), 1.0, 0.0), axis=0, keepdims=True)
    return owner, rank


def order_of(slot, slots):
    npanel = slot.shape[1]
    half = npanel // 2
    core = lax.axis_index("slab") % 2
    place = iota((npanel, npanel), 0)
    wanted = jnp.where(place < half, 2 * place + core, 2 * (place - half) + 1 - core)
    column = jnp.sum(jnp.where(iota((npanel, npanel), 1) == wanted, slot, 0.0), axis=1, keepdims=True)
    return jnp.where(iota((npanel, slots), 1).astype(F32) == column, 1.0, 0.0).astype(BF16)


def select_kernel(cap, ids_ref, vec_ref, pay_ref, over_ref, here_ref, held_ref, block_ref, in_sem, out_sem):
    ids_load = pltpu.make_async_copy(ids_ref, here_ref, in_sem.at[0])
    load = pltpu.make_async_copy(vec_ref, held_ref, in_sem.at[1])
    ids_load.start()
    load.start()
    rows, held, sites = vec_ref.shape
    ids_load.wait()
    ids = here_ref[...]
    npanel = ids.shape[1]
    local = ids - lax.axis_index("vec") * held
    inside = (local >= 0) & (local < held)
    owner, rank = owner_and_rank(ids, pay_ref.shape[0], held)
    over_ref[0] = (jnp.max(rank) >= cap).astype(jnp.int32)
    place = jnp.where(inside, rank, -1.0)
    to_slot = jnp.where(iota((cap, npanel), 0).astype(F32) == place, 1.0, 0.0)
    of_held = jnp.where(iota((held, npanel), 0) == local, 1.0, 0.0)
    pick = lax.dot_general(to_slot, of_held, NT, preferred_element_type=F32).astype(BF16)
    load.wait()
    for row in range(rows):
        block_ref[row * cap:(row + 1) * cap, :] = jnp.dot(
            pick, held_ref[row], preferred_element_type=F32).astype(BF16)
    copies = [pltpu.make_async_copy(block_ref, pay_ref.at[peer], out_sem.at[peer]) for peer in range(pay_ref.shape[0])]
    for copy in copies:
        copy.start()
    for copy in copies:
        copy.wait()


def link_terms(ahead, behind, fore, back):
    real, imag = [], []
    for row in range(3):
        re, im = 0.0, 0.0
        for col in range(3):
            ur, ui = fore(row * 3 + col), fore(9 + row * 3 + col)
            re = re + ur * ahead[col] - ui * ahead[3 + col]
            im = im + ur * ahead[3 + col] + ui * ahead[col]
        for col in range(3):
            ur, ui = back(col * 3 + row), back(9 + col * 3 + row)
            re = re - ur * behind[col] - ui * behind[3 + col]
            im = im - ur * behind[3 + col] + ui * behind[col]
        real.append(re)
        imag.append(im)
    return real + imag


def turn_x(value, ahead):
    inner = iota((value.shape[0], LANES), 1) % LX
    parts = []
    for at in range(0, value.shape[1], LANES):
        part = value[:, at:at + LANES]
        if ahead:
            part = jnp.where(inner == LX - 1, pltpu.roll(part, LX - 1, 1), pltpu.roll(part, LANES - 1, 1))
        else:
            part = jnp.where(inner == 0, pltpu.roll(part, LANES - LX + 1, 1), pltpu.roll(part, 1, 1))
        parts.append(part)
    return jnp.concatenate(parts, axis=1)


def turn_y(value, ahead):
    sites = value.shape[1]
    return pltpu.roll(value, sites - LX if ahead else LX, 1)


def planar_kernel(cap, owners, momenta_ref, ids_ref, vec_ref, links_ref, out_ref, phase_ref, order_ref,
                  link_ref, turned_ref):
    rows, held, sites = vec_ref.shape
    for axis_id, turn in enumerate((turn_x, turn_y)):
        link = links_ref[axis_id].astype(F32) * 0.5
        link_ref[2 * axis_id] = link
        link_ref[2 * axis_id + 1] = turn(link, False)

    def step(at, carry):
        first = pl.multiple_of(at * TILE, TILE)
        for row in range(rows):
            value = vec_ref[row, pl.ds(first, TILE), :].astype(F32)
            for axis_id, turn in enumerate((turn_x, turn_y)):
                turned_ref[axis_id, 0, row] = turn(value, True)
                turned_ref[axis_id, 1, row] = turn(value, False)
        for axis_id in range(2):
            for lane in range(0, sites, LANES):
                span = slice(lane, lane + LANES)
                ahead = [turned_ref[axis_id, 0, row, :, span] for row in range(rows)]
                behind = [turned_ref[axis_id, 1, row, :, span] for row in range(rows)]
                shifted = link_terms(
                    ahead, behind,
                    lambda e: link_ref[2 * axis_id, e:e + 1, span],
                    lambda e: link_ref[2 * axis_id + 1, e:e + 1, span],
                )
                for row in range(rows):
                    out_ref[axis_id, pl.ds(first, TILE), row * sites + lane:row * sites + lane + LANES] = (
                        shifted[row].astype(BF16))
        return carry

    lax.fori_loop(0, held // TILE, step, 0)
    owner, rank = owner_and_rank(ids_ref[...], owners, held)
    fits = jnp.max(rank, axis=1, keepdims=True) < cap
    order_ref[...] = order_of(jnp.where(fits, owner * cap + rank, -1.0), owners * cap)
    nmom = momenta_ref.shape[0]
    slab_id = lax.axis_index("slab")
    modulus = sites * lax.axis_size("slab")
    shape = (2 * nmom, sites)
    site, line = iota(shape, 1), iota(shape, 0)
    x_coord, y_coord = site % LX, site // LX
    turns = jnp.zeros(shape, jnp.int32)
    for mom in range(nmom):
        along = (momenta_ref[mom, 0] * (modulus // LX) * x_coord
                 + momenta_ref[mom, 1] * (modulus // LY) * y_coord
                 + momenta_ref[mom, 2] * sites * slab_id)
        turns = jnp.where(line % nmom == mom, along, turns)
    turns = jnp.where(line >= nmom, turns - modulus // 4, turns) & (modulus - 1)
    turns = jnp.where(turns >= modulus // 2, turns - modulus, turns)
    phase_ref[...] = jnp.cos(turns.astype(F32) * (2.0 * math.pi / modulus))


def height_kernel(planar_ref, links_ref, below_ref, inner_ref, outer_ref, out_ref, link_ref):
    planes, held, width = planar_ref.shape
    out_ref[0:planes * held, :] = planar_ref[...].reshape(planes * held, width)
    first_core = lax.axis_index("slab") % 2 == 0
    pl.when(first_core)(lambda: height(links_ref, below_ref, inner_ref, outer_ref, out_ref, link_ref))
    pl.when(jnp.logical_not(first_core))(lambda: height(links_ref, below_ref, outer_ref, inner_ref, out_ref, link_ref))


def height(links_ref, below_ref, ahead_ref, behind_ref, out_ref, link_ref):
    held = out_ref.shape[0] // 3
    sites = links_ref.shape[2]
    rows = out_ref.shape[1] // sites
    link_ref[0] = links_ref[2].astype(F32) * 0.5
    link_ref[1] = below_ref[2].astype(F32) * 0.5

    def step(at, carry):
        first = pl.multiple_of(at * TILE, TILE)
        for lane in range(0, sites, LANES):
            span = slice(lane, lane + LANES)
            ahead = [ahead_ref[pl.ds(row * held + first, TILE), span].astype(F32) for row in range(rows)]
            behind = [behind_ref[pl.ds(row * held + first, TILE), span].astype(F32) for row in range(rows)]
            shifted = link_terms(
                ahead, behind,
                lambda e: link_ref[0, e:e + 1, span],
                lambda e: link_ref[1, e:e + 1, span],
            )
            for row in range(rows):
                out_ref[pl.ds(2 * held + first, TILE), row * sites + lane:row * sites + lane + LANES] = (
                    shifted[row].astype(BF16))
        return carry

    lax.fori_loop(0, held // TILE, step, 0)


def reorder_kernel(ids_ref, got_ref, out_ref):
    held = got_ref.shape[1] // out_ref.shape[0]
    owners, _, sites = got_ref.shape
    order = order_of(ids_ref[...].astype(F32), owners * held)
    for row in range(out_ref.shape[0]):
        block = got_ref[:, row * held:(row + 1) * held, :].reshape(owners * held, sites)
        out_ref[row] = jnp.dot(order, block, preferred_element_type=F32).astype(BF16)


def main_kernel(cap, half_at, field_ref, phase_ref, order_ref, got_ref, spare_ref,
                out_ref, panel_ref, weight_ref):
    owners = got_ref.shape[0]
    npanel = order_ref.shape[0] // 2
    sites = got_ref.shape[2]
    rows = got_ref.shape[1] // cap
    nmom = phase_ref.shape[0] // 2
    chosen = slice(half_at * npanel, (half_at + 1) * npanel)
    for row in range(rows):
        block = got_ref[:, row * cap:(row + 1) * cap, :].reshape(owners * cap, sites)
        picked = jnp.dot(order_ref[chosen, :], block, preferred_element_type=F32)
        panel_ref[row] = picked + spare_ref[row, chosen, :].astype(F32)

    for first in range(0, npanel, TILE):
        for colour in range(3):
            re = panel_ref[colour, first:first + TILE, :]
            im = panel_ref[3 + colour, first:first + TILE, :]
            for mom in range(nmom):
                cos = phase_ref[mom:mom + 1, :]
                sin = phase_ref[nmom + mom:nmom + mom + 1, :]
                wr = (re * cos - im * sin).astype(BF16)
                wi = re * sin + im * cos
                low = slice(colour * sites, (colour + 1) * sites)
                high = slice((3 + colour) * sites, (4 + colour) * sites)
                at, after = mom * npanel + first, (nmom + mom) * npanel + first
                weight_ref[at:at + TILE, low] = wr
                weight_ref[at:at + TILE, high] = wi.astype(BF16)
                weight_ref[after:after + TILE, low] = (-wi).astype(BF16)
                weight_ref[after:after + TILE, high] = wr
    whole = lax.dot_general(weight_ref[...], field_ref[...], NT, preferred_element_type=F32)
    lines = 2 * nmom + 1
    blocks = [whole[part * npanel:(part + 1) * npanel] for part in range(2 * nmom)]
    for part, block in enumerate(blocks):
        out_ref[pl.ds(part, npanel, stride=lines), :] = block[:, :LANES]
    out_ref[pl.ds(2 * nmom, npanel, stride=lines), :] = jnp.concatenate([b[:, LANES:] for b in blocks], axis=1)


def sum_kernel(nmom, directions_ref, parts_ref, out_ref):
    total = jnp.sum(parts_ref[...], axis=0)
    held = out_ref.shape[-1]
    spill = 3 * held - LANES
    lines = 2 * nmom
    first = jnp.concatenate([total[:, k * LANES:(k + 1) * LANES] for k in range(lines)], axis=0)
    last = total[:, lines * LANES:]
    last = jnp.concatenate([last[:, k * spill:(k + 1) * spill] for k in range(lines)], axis=0)
    total = jnp.concatenate([first, last], axis=1)
    for place in range(out_ref.shape[1]):
        chosen = total[:, 0:held]
        for axis_id in (1, 2):
            along = total[:, axis_id * held:(axis_id + 1) * held]
            chosen = jnp.where(directions_ref[:, place:place + 1] == axis_id, along, chosen)
        out_ref[0, place] = chosen[:nmom]
        out_ref[1, place] = chosen[nmom:]


def specs(*spaces):
    kinds = {"s": pltpu.SMEM, "v": pltpu.VMEM, "a": pl.ANY, "h": pltpu.HBM}
    return [pl.BlockSpec(memory_space=kinds[space]) for space in spaces]


def call(kernel, out_shape, ins, outs, name, scratch=(), cost=0):
    return pl.pallas_call(
        kernel, out_shape=out_shape, in_specs=specs(*ins), out_specs=specs(*outs),
        scratch_shapes=list(scratch), name=name,
        cost_estimate=pl.CostEstimate(flops=cost, bytes_accessed=0, transcendentals=0) if cost else None,
        compiler_params=pltpu.CompilerParams(vmem_limit_bytes=16 * 1024 * 1024),
    )


def in_vmem(value):
    return pltpu.with_memory_space_constraint(value, pltpu.VMEM)


def body(vectors, links, momenta, directions, panel_index):
    rows, held, planes, sites = vectors.shape
    npanel = panel_index.shape[0]
    nmom = momenta.shape[0]
    nslab, nvec = lax.axis_size("slab"), lax.axis_size("vec")
    half = npanel // 2
    lines = 2 * nmom + 1
    vec = vectors.reshape(rows, held, sites)
    link = links.reshape(3, 18, sites)
    ids = panel_index.reshape(1, npanel)
    shape = jax.ShapeDtypeStruct
    vm = pltpu.VMEM
    flat = vec.reshape(rows * held, sites)
    mate = [(i, i ^ 1) for i in range(nslab)]
    beyond = [(i, (i + 1) % nslab if i % 2 else (i - 1) % nslab) for i in range(nslab)]
    upward = [(i, (i + 1) % nslab) for i in range(nslab)]
    outer = lax.ppermute(flat, "slab", beyond)
    pay, over = call(
        functools.partial(select_kernel, CAP), [shape((nvec, rows * CAP, sites), BF16), pltpu.SMEM((1,), jnp.int32)],
        "hh", "as", "select",
        [vm(ids.shape, jnp.int32), vm(vec.shape, BF16), vm((rows * CAP, sites), BF16), pltpu.SemaphoreType.DMA((2,)),
         pltpu.SemaphoreType.DMA((nvec,))],
        COST,
    )(ids, vec)
    got = lax.all_to_all(pay, "vec", 0, 0, tiled=True)
    def gather_all():
        every = jnp.broadcast_to(vec.reshape(1, rows * held, sites), (nvec, rows * held, sites))
        every = lax.all_to_all(every, "vec", 0, 0, tiled=True)
        return call(reorder_kernel, [shape((rows, npanel, sites), BF16)], "vv", "v", "reorder")(ids, every)[0]

    planar, phase, order = call(
        functools.partial(planar_kernel, CAP, nvec),
        [shape((2, held, rows * sites), BF16), shape((2 * nmom, sites), F32), shape((npanel, nvec * CAP), BF16)],
        "svvv", "vvv", "planar",
        [vm((4, 18, sites), F32), vm((2, 2, rows, TILE, sites), F32)], COST,
    )(momenta, ids, vec, link)
    spare = lax.cond(over[0] != 0, gather_all, lambda: jnp.zeros((rows, npanel, sites), BF16))
    outer, flat_late, link_late = lax.optimization_barrier((outer, flat, link))
    inner = lax.ppermute(flat_late, "slab", mate)
    below = lax.ppermute(link_late, "slab", upward)
    field = call(
        height_kernel, [shape((3 * held, rows * sites), BF16)], "vvvvv", "v", "height", [vm((2, 18, sites), F32)],
    )(planar, link, below, inner, outer)[0]
    part = shape((half * lines, LANES), F32)
    inputs = (field, in_vmem(phase), in_vmem(order), got, in_vmem(spare))
    send, keep = [
        call(
            functools.partial(main_kernel, CAP, half_at), [part], "vvvvv", "v", name,
            [vm((rows, half, sites), F32),
             vm((2 * nmom * half, rows * sites), BF16)],
            cost,
        )(*inputs)[0]
        for half_at, name, cost in ((1, "send", 0), (0, "keep", COST))
    ]
    pair = lax.ppermute(send, "slab", mate)
    groups = [[2 * k + c for k in range(nslab // 2)] for c in range(2)]
    both = (keep + pair).reshape(half, 1, lines * LANES)
    parts = lax.all_to_all(both, "slab", 0, 0, axis_index_groups=groups, tiled=True)
    return call(
        functools.partial(sum_kernel, nmom), [shape((2, 3, nmom, held), F32)], "vv", "v", "total",
    )(in_vmem(directions.reshape(1, 3)), parts)[0][None]


def solution(mesh):
    placed = (P(None, "vec", "slab", None), P(None, None, "slab", None), P(), P(), P())
    return jax.shard_map(
        body,
        mesh=mesh,
        in_specs=placed,
        out_specs=P("slab", None, None, None, "vec"),
        check_vma=False,
    )
```

```python
import functools
import math

import jax
import jax.numpy as jnp
from jax import lax
from jax.experimental import pallas as pl
from jax.experimental.pallas import tpu as pltpu
from jax.sharding import PartitionSpec as P

LX = 32
LY = 16
CAP = 16
COST = 50_000_000_000
TILE = 16
LANES = 128
F32 = jnp.float32
BF16 = jnp.bfloat16
NT = (((1,), (1,)), ((), ()))


def iota(shape, dim):
    return lax.broadcasted_iota(jnp.int32, shape, dim)


def as_column(row):
    n = row.shape[1]
    return jnp.sum(jnp.where(iota((n, n), 0) == iota((n, n), 1), row, 0.0), axis=1, keepdims=True)


def owner_and_rank(ids, owners, held):
    npanel = ids.shape[1]
    owner = jnp.zeros(ids.shape, F32)
    for other in range(1, owners):
        owner = owner + jnp.where(ids >= other * held, 1.0, 0.0)
    before = iota((npanel, npanel), 0) < iota((npanel, npanel), 1)
    rank = jnp.sum(jnp.where(before & (as_column(owner) == owner), 1.0, 0.0), axis=0, keepdims=True)
    return owner, rank


def order_of(slot, slots):
    npanel = slot.shape[1]
    half = npanel // 2
    core = lax.axis_index("slab") % 2
    place = iota((npanel, npanel), 0)
    wanted = jnp.where(place < half, 2 * place + core, 2 * (place - half) + 1 - core)
    column = jnp.sum(jnp.where(iota((npanel, npanel), 1) == wanted, slot, 0.0), axis=1, keepdims=True)
    return jnp.where(iota((npanel, slots), 1).astype(F32) == column, 1.0, 0.0).astype(BF16)


def select_kernel(cap, ids_ref, vec_ref, pay_ref, over_ref, here_ref, held_ref, block_ref, in_sem, out_sem):
    ids_load = pltpu.make_async_copy(ids_ref, here_ref, in_sem.at[0])
    load = pltpu.make_async_copy(vec_ref, held_ref, in_sem.at[1])
    ids_load.start()
    load.start()
    rows, held, sites = vec_ref.shape
    ids_load.wait()
    ids = here_ref[...]
    npanel = ids.shape[1]
    local = ids - lax.axis_index("vec") * held
    inside = (local >= 0) & (local < held)
    owner, rank = owner_and_rank(ids, pay_ref.shape[0], held)
    over_ref[0] = (jnp.max(rank) >= cap).astype(jnp.int32)
    place = jnp.where(inside, rank, -1.0)
    to_slot = jnp.where(iota((cap, npanel), 0).astype(F32) == place, 1.0, 0.0)
    of_held = jnp.where(iota((held, npanel), 0) == local, 1.0, 0.0)
    pick = lax.dot_general(to_slot, of_held, NT, preferred_element_type=F32).astype(BF16)
    load.wait()
    for row in range(rows):
        block_ref[row * cap:(row + 1) * cap, :] = jnp.dot(
            pick, held_ref[row], preferred_element_type=F32).astype(BF16)
    copies = [pltpu.make_async_copy(block_ref, pay_ref.at[peer], out_sem.at[peer]) for peer in range(pay_ref.shape[0])]
    for copy in copies:
        copy.start()
    for copy in copies:
        copy.wait()


def link_terms(ahead, behind, fore, back):
    real, imag = [], []
    for row in range(3):
        re, im = 0.0, 0.0
        for col in range(3):
            ur, ui = fore(row * 3 + col), fore(9 + row * 3 + col)
            re = re + ur * ahead[col] - ui * ahead[3 + col]
            im = im + ur * ahead[3 + col] + ui * ahead[col]
        for col in range(3):
            ur, ui = back(col * 3 + row), back(9 + col * 3 + row)
            re = re - ur * behind[col] - ui * behind[3 + col]
            im = im - ur * behind[3 + col] + ui * behind[col]
        real.append(re)
        imag.append(im)
    return real + imag


def turn_x(value, ahead):
    inner = iota((value.shape[0], LANES), 1) % LX
    parts = []
    for at in range(0, value.shape[1], LANES):
        part = value[:, at:at + LANES]
        if ahead:
            part = jnp.where(inner == LX - 1, pltpu.roll(part, LX - 1, 1), pltpu.roll(part, LANES - 1, 1))
        else:
            part = jnp.where(inner == 0, pltpu.roll(part, LANES - LX + 1, 1), pltpu.roll(part, 1, 1))
        parts.append(part)
    return jnp.concatenate(parts, axis=1)


def turn_y(value, ahead):
    sites = value.shape[1]
    return pltpu.roll(value, sites - LX if ahead else LX, 1)


def planar_kernel(cap, owners, momenta_ref, ids_ref, vec_ref, links_ref, out_ref, phase_ref, order_ref,
                  link_ref, turned_ref):
    rows, held, sites = vec_ref.shape
    for axis_id, turn in enumerate((turn_x, turn_y)):
        link = links_ref[axis_id].astype(F32) * 0.5
        link_ref[2 * axis_id] = link
        link_ref[2 * axis_id + 1] = turn(link, False)

    def step(at, carry):
        first = pl.multiple_of(at * TILE, TILE)
        for row in range(rows):
            value = vec_ref[row, pl.ds(first, TILE), :].astype(F32)
            for axis_id, turn in enumerate((turn_x, turn_y)):
                turned_ref[axis_id, 0, row] = turn(value, True)
                turned_ref[axis_id, 1, row] = turn(value, False)
        for axis_id in range(2):
            for lane in range(0, sites, LANES):
                span = slice(lane, lane + LANES)
                ahead = [turned_ref[axis_id, 0, row, :, span] for row in range(rows)]
                behind = [turned_ref[axis_id, 1, row, :, span] for row in range(rows)]
                shifted = link_terms(
                    ahead, behind,
                    lambda e: link_ref[2 * axis_id, e:e + 1, span],
                    lambda e: link_ref[2 * axis_id + 1, e:e + 1, span],
                )
                for row in range(rows):
                    out_ref[axis_id, pl.ds(first, TILE), row * sites + lane:row * sites + lane + LANES] = (
                        shifted[row].astype(BF16))
        return carry

    lax.fori_loop(0, held // TILE, step, 0)
    owner, rank = owner_and_rank(ids_ref[...], owners, held)
    fits = jnp.max(rank, axis=1, keepdims=True) < cap
    order_ref[...] = order_of(jnp.where(fits, owner * cap + rank, -1.0), owners * cap)
    nmom = momenta_ref.shape[0]
    slab_id = lax.axis_index("slab")
    modulus = sites * lax.axis_size("slab")
    shape = (2 * nmom, sites)
    site, line = iota(shape, 1), iota(shape, 0)
    x_coord, y_coord = site % LX, site // LX
    turns = jnp.zeros(shape, jnp.int32)
    for mom in range(nmom):
        along = (momenta_ref[mom, 0] * (modulus // LX) * x_coord
                 + momenta_ref[mom, 1] * (modulus // LY) * y_coord
                 + momenta_ref[mom, 2] * sites * slab_id)
        turns = jnp.where(line % nmom == mom, along, turns)
    turns = jnp.where(line >= nmom, turns - modulus // 4, turns) & (modulus - 1)
    turns = jnp.where(turns >= modulus // 2, turns - modulus, turns)
    phase_ref[...] = jnp.cos(turns.astype(F32) * (2.0 * math.pi / modulus))


def height_kernel(planar_ref, links_ref, below_ref, inner_ref, outer_ref, out_ref, link_ref):
    planes, held, width = planar_ref.shape
    out_ref[0:planes * held, :] = planar_ref[...].reshape(planes * held, width)
    first_core = lax.axis_index("slab") % 2 == 0
    pl.when(first_core)(lambda: height(links_ref, below_ref, inner_ref, outer_ref, out_ref, link_ref))
    pl.when(jnp.logical_not(first_core))(lambda: height(links_ref, below_ref, outer_ref, inner_ref, out_ref, link_ref))


def height(links_ref, below_ref, ahead_ref, behind_ref, out_ref, link_ref):
    held = out_ref.shape[0] // 3
    sites = links_ref.shape[2]
    rows = out_ref.shape[1] // sites
    link_ref[0] = links_ref[2].astype(F32) * 0.5
    link_ref[1] = below_ref[...].astype(F32) * 0.5

    def step(at, carry):
        first = pl.multiple_of(at * TILE, TILE)
        for lane in range(0, sites, LANES):
            span = slice(lane, lane + LANES)
            ahead = [ahead_ref[pl.ds(row * held + first, TILE), span].astype(F32) for row in range(rows)]
            behind = [behind_ref[pl.ds(row * held + first, TILE), span].astype(F32) for row in range(rows)]
            shifted = link_terms(
                ahead, behind,
                lambda e: link_ref[0, e:e + 1, span],
                lambda e: link_ref[1, e:e + 1, span],
            )
            for row in range(rows):
                out_ref[pl.ds(2 * held + first, TILE), row * sites + lane:row * sites + lane + LANES] = (
                    shifted[row].astype(BF16))
        return carry

    lax.fori_loop(0, held // TILE, step, 0)


def reorder_kernel(ids_ref, got_ref, out_ref):
    held = got_ref.shape[1] // out_ref.shape[0]
    owners, _, sites = got_ref.shape
    order = order_of(ids_ref[...].astype(F32), owners * held)
    for row in range(out_ref.shape[0]):
        block = got_ref[:, row * held:(row + 1) * held, :].reshape(owners * held, sites)
        out_ref[row] = jnp.dot(order, block, preferred_element_type=F32).astype(BF16)


def main_kernel(cap, half_at, field_ref, phase_ref, order_ref, got_ref, spare_ref,
                out_ref, panel_ref, weight_ref):
    owners = got_ref.shape[0]
    npanel = order_ref.shape[0] // 2
    sites = got_ref.shape[2]
    rows = got_ref.shape[1] // cap
    nmom = phase_ref.shape[0] // 2
    chosen = slice(half_at * npanel, (half_at + 1) * npanel)
    for row in range(rows):
        block = got_ref[:, row * cap:(row + 1) * cap, :].reshape(owners * cap, sites)
        picked = jnp.dot(order_ref[chosen, :], block, preferred_element_type=F32)
        panel_ref[row] = picked + spare_ref[row, chosen, :].astype(F32)

    for first in range(0, npanel, TILE):
        for colour in range(3):
            re = panel_ref[colour, first:first + TILE, :]
            im = panel_ref[3 + colour, first:first + TILE, :]
            for mom in range(nmom):
                cos = phase_ref[mom:mom + 1, :]
                sin = phase_ref[nmom + mom:nmom + mom + 1, :]
                wr = (re * cos - im * sin).astype(BF16)
                wi = re * sin + im * cos
                low = slice(colour * sites, (colour + 1) * sites)
                high = slice((3 + colour) * sites, (4 + colour) * sites)
                at, after = mom * npanel + first, (nmom + mom) * npanel + first
                weight_ref[at:at + TILE, low] = wr
                weight_ref[at:at + TILE, high] = wi.astype(BF16)
                weight_ref[after:after + TILE, low] = (-wi).astype(BF16)
                weight_ref[after:after + TILE, high] = wr
    whole = lax.dot_general(weight_ref[...], field_ref[...], NT, preferred_element_type=F32)
    lines = 2 * nmom + 1
    blocks = [whole[part * npanel:(part + 1) * npanel] for part in range(2 * nmom)]
    for part, block in enumerate(blocks):
        out_ref[pl.ds(part, npanel, stride=lines), :] = block[:, :LANES]
    out_ref[pl.ds(2 * nmom, npanel, stride=lines), :] = jnp.concatenate([b[:, LANES:] for b in blocks], axis=1)


def sum_kernel(nmom, directions_ref, parts_ref, out_ref):
    total = jnp.sum(parts_ref[...], axis=0)
    held = out_ref.shape[-1]
    spill = 3 * held - LANES
    lines = 2 * nmom
    first = jnp.concatenate([total[:, k * LANES:(k + 1) * LANES] for k in range(lines)], axis=0)
    last = total[:, lines * LANES:]
    last = jnp.concatenate([last[:, k * spill:(k + 1) * spill] for k in range(lines)], axis=0)
    total = jnp.concatenate([first, last], axis=1)
    for place in range(out_ref.shape[1]):
        chosen = total[:, 0:held]
        for axis_id in (1, 2):
            along = total[:, axis_id * held:(axis_id + 1) * held]
            chosen = jnp.where(directions_ref[:, place:place + 1] == axis_id, along, chosen)
        out_ref[0, place] = chosen[:nmom]
        out_ref[1, place] = chosen[nmom:]


def specs(*spaces):
    kinds = {"s": pltpu.SMEM, "v": pltpu.VMEM, "a": pl.ANY, "h": pltpu.HBM}
    return [pl.BlockSpec(memory_space=kinds[space]) for space in spaces]


def call(kernel, out_shape, ins, outs, name, scratch=(), cost=0):
    return pl.pallas_call(
        kernel, out_shape=out_shape, in_specs=specs(*ins), out_specs=specs(*outs),
        scratch_shapes=list(scratch), name=name,
        cost_estimate=pl.CostEstimate(flops=cost, bytes_accessed=0, transcendentals=0) if cost else None,
        compiler_params=pltpu.CompilerParams(vmem_limit_bytes=16 * 1024 * 1024),
    )


def in_vmem(value):
    return pltpu.with_memory_space_constraint(value, pltpu.VMEM)


def body(vectors, links, momenta, directions, panel_index):
    rows, held, planes, sites = vectors.shape
    npanel = panel_index.shape[0]
    nmom = momenta.shape[0]
    nslab, nvec = lax.axis_size("slab"), lax.axis_size("vec")
    half = npanel // 2
    lines = 2 * nmom + 1
    vec = vectors.reshape(rows, held, sites)
    link = links.reshape(3, 18, sites)
    ids = panel_index.reshape(1, npanel)
    shape = jax.ShapeDtypeStruct
    vm = pltpu.VMEM
    flat = vec.reshape(rows * held, sites)
    mate = [(i, i ^ 1) for i in range(nslab)]
    beyond = [(i, (i + 1) % nslab if i % 2 else (i - 1) % nslab) for i in range(nslab)]
    upward = [(i, (i + 1) % nslab) for i in range(nslab)]
    outer = lax.ppermute(flat, "slab", beyond)
    pay, over = call(
        functools.partial(select_kernel, CAP), [shape((nvec, rows * CAP, sites), BF16), pltpu.SMEM((1,), jnp.int32)],
        "hh", "as", "select",
        [vm(ids.shape, jnp.int32), vm(vec.shape, BF16), vm((rows * CAP, sites), BF16), pltpu.SemaphoreType.DMA((2,)),
         pltpu.SemaphoreType.DMA((nvec,))],
        COST,
    )(ids, vec)
    got = lax.all_to_all(pay, "vec", 0, 0, tiled=True)
    def gather_all():
        every = jnp.broadcast_to(vec.reshape(1, rows * held, sites), (nvec, rows * held, sites))
        every = lax.all_to_all(every, "vec", 0, 0, tiled=True)
        return call(reorder_kernel, [shape((rows, npanel, sites), BF16)], "vv", "v", "reorder")(ids, every)[0]

    planar, phase, order = call(
        functools.partial(planar_kernel, CAP, nvec),
        [shape((2, held, rows * sites), BF16), shape((2 * nmom, sites), F32), shape((npanel, nvec * CAP), BF16)],
        "svvv", "vvv", "planar",
        [vm((4, 18, sites), F32), vm((2, 2, rows, TILE, sites), F32)], COST,
    )(momenta, ids, vec, link)
    spare = lax.cond(over[0] != 0, gather_all, lambda: jnp.zeros((rows, npanel, sites), BF16))
    outer, flat_late, link_late = lax.optimization_barrier((outer, flat, link))
    inner = lax.ppermute(flat_late, "slab", mate)
    below = lax.ppermute(link_late[2], "slab", upward)
    field = call(
        height_kernel, [shape((3 * held, rows * sites), BF16)], "vvvvv", "v", "height", [vm((2, 18, sites), F32)],
    )(planar, link, below, inner, outer)[0]
    part = shape((half * lines, LANES), F32)
    inputs = (field, in_vmem(phase), in_vmem(order), got, in_vmem(spare))
    send, keep = [
        call(
            functools.partial(main_kernel, CAP, half_at), [part], "vvvvv", "v", name,
            [vm((rows, half, sites), F32),
             vm((2 * nmom * half, rows * sites), BF16)],
            cost,
        )(*inputs)[0]
        for half_at, name, cost in ((1, "send", 0), (0, "keep", COST))
    ]
    pair = lax.ppermute(send, "slab", mate)
    groups = [[2 * k + c for k in range(nslab // 2)] for c in range(2)]
    both = (keep + pair).reshape(half, 1, lines * LANES)
    parts = lax.all_to_all(both, "slab", 0, 0, axis_index_groups=groups, tiled=True)
    return call(
        functools.partial(sum_kernel, nmom), [shape((2, 3, nmom, held), F32)], "vv", "v", "total",
    )(in_vmem(directions.reshape(1, 3)), parts)[0][None]


def solution(mesh):
    placed = (P(None, "vec", "slab", None), P(None, None, "slab", None), P(), P(), P())
    return jax.shard_map(
        body,
        mesh=mesh,
        in_specs=placed,
        out_specs=P("slab", None, None, None, "vec"),
        check_vma=False,
    )
```

```python
import functools
import math

import jax
import jax.numpy as jnp
from jax import lax
from jax.experimental import pallas as pl
from jax.experimental.pallas import tpu as pltpu
from jax.sharding import PartitionSpec as P

LX = 32
LY = 16
CAP = 16
COST = 50_000_000_000
TILE = 16
LANES = 128
F32 = jnp.float32
BF16 = jnp.bfloat16
NT = (((1,), (1,)), ((), ()))


def iota(shape, dim):
    return lax.broadcasted_iota(jnp.int32, shape, dim)


def as_column(row):
    n = row.shape[1]
    return jnp.sum(jnp.where(iota((n, n), 0) == iota((n, n), 1), row, 0.0), axis=1, keepdims=True)


def owner_and_rank(ids, owners, held):
    npanel = ids.shape[1]
    owner = jnp.zeros(ids.shape, F32)
    for other in range(1, owners):
        owner = owner + jnp.where(ids >= other * held, 1.0, 0.0)
    before = iota((npanel, npanel), 0) < iota((npanel, npanel), 1)
    rank = jnp.sum(jnp.where(before & (as_column(owner) == owner), 1.0, 0.0), axis=0, keepdims=True)
    return owner, rank


def order_of(slot, slots):
    npanel = slot.shape[1]
    half = npanel // 2
    core = lax.axis_index("slab") % 2
    place = iota((npanel, npanel), 0)
    wanted = jnp.where(place < half, 2 * place + core, 2 * (place - half) + 1 - core)
    column = jnp.sum(jnp.where(iota((npanel, npanel), 1) == wanted, slot, 0.0), axis=1, keepdims=True)
    return jnp.where(iota((npanel, slots), 1).astype(F32) == column, 1.0, 0.0).astype(BF16)


def select_kernel(cap, ids_ref, vec_ref, pay_ref, over_ref, here_ref, held_ref, in_sem):
    ids_load = pltpu.make_async_copy(ids_ref, here_ref, in_sem.at[0])
    load = pltpu.make_async_copy(vec_ref, held_ref, in_sem.at[1])
    ids_load.start()
    load.start()
    rows, held, sites = vec_ref.shape
    ids_load.wait()
    ids = here_ref[...]
    npanel = ids.shape[1]
    local = ids - lax.axis_index("vec") * held
    inside = (local >= 0) & (local < held)
    owner, rank = owner_and_rank(ids, pay_ref.shape[0], held)
    over_ref[0] = (jnp.max(rank) >= cap).astype(jnp.int32)
    place = jnp.where(inside, rank, -1.0)
    to_slot = jnp.where(iota((cap, npanel), 0).astype(F32) == place, 1.0, 0.0)
    of_held = jnp.where(iota((held, npanel), 0) == local, 1.0, 0.0)
    pick = lax.dot_general(to_slot, of_held, NT, preferred_element_type=F32).astype(BF16)
    load.wait()
    for row in range(rows):
        part = jnp.dot(pick, held_ref[row], preferred_element_type=F32).astype(BF16)
        for peer in range(pay_ref.shape[0]):
            pay_ref[peer, row * cap:(row + 1) * cap, :] = part


def link_terms(ahead, behind, fore, back):
    real, imag = [], []
    for row in range(3):
        re, im = 0.0, 0.0
        for col in range(3):
            ur, ui = fore(row * 3 + col), fore(9 + row * 3 + col)
            re = re + ur * ahead[col] - ui * ahead[3 + col]
            im = im + ur * ahead[3 + col] + ui * ahead[col]
        for col in range(3):
            ur, ui = back(col * 3 + row), back(9 + col * 3 + row)
            re = re - ur * behind[col] - ui * behind[3 + col]
            im = im - ur * behind[3 + col] + ui * behind[col]
        real.append(re)
        imag.append(im)
    return real + imag


def turn_x(value, ahead):
    inner = iota((value.shape[0], LANES), 1) % LX
    parts = []
    for at in range(0, value.shape[1], LANES):
        part = value[:, at:at + LANES]
        if ahead:
            part = jnp.where(inner == LX - 1, pltpu.roll(part, LX - 1, 1), pltpu.roll(part, LANES - 1, 1))
        else:
            part = jnp.where(inner == 0, pltpu.roll(part, LANES - LX + 1, 1), pltpu.roll(part, 1, 1))
        parts.append(part)
    return jnp.concatenate(parts, axis=1)


def turn_y(value, ahead):
    sites = value.shape[1]
    return pltpu.roll(value, sites - LX if ahead else LX, 1)


def planar_kernel(cap, owners, momenta_ref, ids_ref, vec_ref, links_ref, out_ref, phase_ref, order_ref,
                  link_ref, turned_ref):
    rows, held, sites = vec_ref.shape
    for axis_id, turn in enumerate((turn_x, turn_y)):
        link = links_ref[axis_id].astype(F32) * 0.5
        link_ref[2 * axis_id] = link
        link_ref[2 * axis_id + 1] = turn(link, False)

    def step(at, carry):
        first = pl.multiple_of(at * TILE, TILE)
        for row in range(rows):
            value = vec_ref[row, pl.ds(first, TILE), :].astype(F32)
            for axis_id, turn in enumerate((turn_x, turn_y)):
                turned_ref[axis_id, 0, row] = turn(value, True)
                turned_ref[axis_id, 1, row] = turn(value, False)
        for axis_id in range(2):
            for lane in range(0, sites, LANES):
                span = slice(lane, lane + LANES)
                ahead = [turned_ref[axis_id, 0, row, :, span] for row in range(rows)]
                behind = [turned_ref[axis_id, 1, row, :, span] for row in range(rows)]
                shifted = link_terms(
                    ahead, behind,
                    lambda e: link_ref[2 * axis_id, e:e + 1, span],
                    lambda e: link_ref[2 * axis_id + 1, e:e + 1, span],
                )
                for row in range(rows):
                    out_ref[axis_id, pl.ds(first, TILE), row * sites + lane:row * sites + lane + LANES] = (
                        shifted[row].astype(BF16))
        return carry

    lax.fori_loop(0, held // TILE, step, 0)
    owner, rank = owner_and_rank(ids_ref[...], owners, held)
    fits = jnp.max(rank, axis=1, keepdims=True) < cap
    order_ref[...] = order_of(jnp.where(fits, owner * cap + rank, -1.0), owners * cap)
    nmom = momenta_ref.shape[0]
    slab_id = lax.axis_index("slab")
    modulus = sites * lax.axis_size("slab")
    shape = (2 * nmom, sites)
    site, line = iota(shape, 1), iota(shape, 0)
    x_coord, y_coord = site % LX, site // LX
    turns = jnp.zeros(shape, jnp.int32)
    for mom in range(nmom):
        along = (momenta_ref[mom, 0] * (modulus // LX) * x_coord
                 + momenta_ref[mom, 1] * (modulus // LY) * y_coord
                 + momenta_ref[mom, 2] * sites * slab_id)
        turns = jnp.where(line % nmom == mom, along, turns)
    turns = jnp.where(line >= nmom, turns - modulus // 4, turns) & (modulus - 1)
    turns = jnp.where(turns >= modulus // 2, turns - modulus, turns)
    phase_ref[...] = jnp.cos(turns.astype(F32) * (2.0 * math.pi / modulus))


def height_kernel(planar_ref, links_ref, below_ref, inner_ref, outer_ref, out_ref, link_ref):
    planes, held, width = planar_ref.shape
    out_ref[0:planes * held, :] = planar_ref[...].reshape(planes * held, width)
    first_core = lax.axis_index("slab") % 2 == 0
    pl.when(first_core)(lambda: height(links_ref, below_ref, inner_ref, outer_ref, out_ref, link_ref))
    pl.when(jnp.logical_not(first_core))(lambda: height(links_ref, below_ref, outer_ref, inner_ref, out_ref, link_ref))


def height(links_ref, below_ref, ahead_ref, behind_ref, out_ref, link_ref):
    held = out_ref.shape[0] // 3
    sites = links_ref.shape[2]
    rows = out_ref.shape[1] // sites
    link_ref[0] = links_ref[2].astype(F32) * 0.5
    link_ref[1] = below_ref[...].astype(F32) * 0.5

    def step(at, carry):
        first = pl.multiple_of(at * TILE, TILE)
        for lane in range(0, sites, LANES):
            span = slice(lane, lane + LANES)
            ahead = [ahead_ref[pl.ds(row * held + first, TILE), span].astype(F32) for row in range(rows)]
            behind = [behind_ref[pl.ds(row * held + first, TILE), span].astype(F32) for row in range(rows)]
            shifted = link_terms(
                ahead, behind,
                lambda e: link_ref[0, e:e + 1, span],
                lambda e: link_ref[1, e:e + 1, span],
            )
            for row in range(rows):
                out_ref[pl.ds(2 * held + first, TILE), row * sites + lane:row * sites + lane + LANES] = (
                    shifted[row].astype(BF16))
        return carry

    lax.fori_loop(0, held // TILE, step, 0)


def reorder_kernel(ids_ref, got_ref, out_ref):
    held = got_ref.shape[1] // out_ref.shape[0]
    owners, _, sites = got_ref.shape
    order = order_of(ids_ref[...].astype(F32), owners * held)
    for row in range(out_ref.shape[0]):
        block = got_ref[:, row * held:(row + 1) * held, :].reshape(owners * held, sites)
        out_ref[row] = jnp.dot(order, block, preferred_element_type=F32).astype(BF16)


def main_kernel(cap, half_at, field_ref, phase_ref, order_ref, got_ref, spare_ref,
                out_ref, panel_ref, weight_ref):
    owners = got_ref.shape[0]
    npanel = order_ref.shape[0] // 2
    sites = got_ref.shape[2]
    rows = got_ref.shape[1] // cap
    nmom = phase_ref.shape[0] // 2
    chosen = slice(half_at * npanel, (half_at + 1) * npanel)
    for row in range(rows):
        block = got_ref[:, row * cap:(row + 1) * cap, :].reshape(owners * cap, sites)
        picked = jnp.dot(order_ref[chosen, :], block, preferred_element_type=F32)
        panel_ref[row] = picked + spare_ref[row, chosen, :].astype(F32)

    for first in range(0, npanel, TILE):
        for colour in range(3):
            re = panel_ref[colour, first:first + TILE, :]
            im = panel_ref[3 + colour, first:first + TILE, :]
            for mom in range(nmom):
                cos = phase_ref[mom:mom + 1, :]
                sin = phase_ref[nmom + mom:nmom + mom + 1, :]
                wr = (re * cos - im * sin).astype(BF16)
                wi = re * sin + im * cos
                low = slice(colour * sites, (colour + 1) * sites)
                high = slice((3 + colour) * sites, (4 + colour) * sites)
                at, after = mom * npanel + first, (nmom + mom) * npanel + first
                weight_ref[at:at + TILE, low] = wr
                weight_ref[at:at + TILE, high] = wi.astype(BF16)
                weight_ref[after:after + TILE, low] = (-wi).astype(BF16)
                weight_ref[after:after + TILE, high] = wr
    whole = lax.dot_general(weight_ref[...], field_ref[...], NT, preferred_element_type=F32)
    lines = 2 * nmom + 1
    blocks = [whole[part * npanel:(part + 1) * npanel] for part in range(2 * nmom)]
    for part, block in enumerate(blocks):
        out_ref[pl.ds(part, npanel, stride=lines), :] = block[:, :LANES]
    out_ref[pl.ds(2 * nmom, npanel, stride=lines), :] = jnp.concatenate([b[:, LANES:] for b in blocks], axis=1)


def sum_kernel(nmom, directions_ref, parts_ref, out_ref):
    held = out_ref.shape[-1]
    spill = 3 * held - LANES
    lines = 2 * nmom
    count = parts_ref.shape[0] // (lines + 1)
    summed = [
        jnp.sum(parts_ref[pl.ds(k, count, stride=lines + 1), :], axis=0, keepdims=True) for k in range(lines + 1)
    ]
    first = jnp.concatenate(summed[:lines], axis=0)
    last = summed[lines]
    last = jnp.concatenate([last[:, k * spill:(k + 1) * spill] for k in range(lines)], axis=0)
    total = jnp.concatenate([first, last], axis=1)
    for place in range(out_ref.shape[1]):
        chosen = total[:, 0:held]
        for axis_id in (1, 2):
            along = total[:, axis_id * held:(axis_id + 1) * held]
            chosen = jnp.where(directions_ref[:, place:place + 1] == axis_id, along, chosen)
        out_ref[0, place] = chosen[:nmom]
        out_ref[1, place] = chosen[nmom:]


def specs(*spaces):
    kinds = {"s": pltpu.SMEM, "v": pltpu.VMEM, "a": pl.ANY, "h": pltpu.HBM}
    return [pl.BlockSpec(memory_space=kinds[space]) for space in spaces]


def call(kernel, out_shape, ins, outs, name, scratch=(), cost=0):
    return pl.pallas_call(
        kernel, out_shape=out_shape, in_specs=specs(*ins), out_specs=specs(*outs),
        scratch_shapes=list(scratch), name=name,
        cost_estimate=pl.CostEstimate(flops=cost, bytes_accessed=0, transcendentals=0) if cost else None,
        compiler_params=pltpu.CompilerParams(vmem_limit_bytes=16 * 1024 * 1024),
    )


def in_vmem(value):
    return pltpu.with_memory_space_constraint(value, pltpu.VMEM)


def body(vectors, links, momenta, directions, panel_index):
    rows, held, planes, sites = vectors.shape
    npanel = panel_index.shape[0]
    nmom = momenta.shape[0]
    nslab, nvec = lax.axis_size("slab"), lax.axis_size("vec")
    half = npanel // 2
    lines = 2 * nmom + 1
    vec = vectors.reshape(rows, held, sites)
    link = links.reshape(3, 18, sites)
    ids = panel_index.reshape(1, npanel)
    shape = jax.ShapeDtypeStruct
    vm = pltpu.VMEM
    flat = vec.reshape(rows * held, sites)
    mate = [(i, i ^ 1) for i in range(nslab)]
    beyond = [(i, (i + 1) % nslab if i % 2 else (i - 1) % nslab) for i in range(nslab)]
    upward = [(i, (i + 1) % nslab) for i in range(nslab)]
    outer = lax.ppermute(flat, "slab", beyond)
    pay, over = call(
        functools.partial(select_kernel, CAP), [shape((nvec, rows * CAP, sites), BF16), pltpu.SMEM((1,), jnp.int32)],
        "hh", "vs", "select",
        [vm(ids.shape, jnp.int32), vm(vec.shape, BF16), pltpu.SemaphoreType.DMA((2,))],
        COST,
    )(ids, vec)
    got = lax.all_to_all(pay, "vec", 0, 0, tiled=True)
    def gather_all():
        every = jnp.broadcast_to(vec.reshape(1, rows * held, sites), (nvec, rows * held, sites))
        every = lax.all_to_all(every, "vec", 0, 0, tiled=True)
        return call(reorder_kernel, [shape((rows, npanel, sites), BF16)], "vv", "v", "reorder")(ids, every)[0]

    planar, phase, order = call(
        functools.partial(planar_kernel, CAP, nvec),
        [shape((2, held, rows * sites), BF16), shape((2 * nmom, sites), F32), shape((npanel, nvec * CAP), BF16)],
        "svvv", "vvv", "planar",
        [vm((4, 18, sites), F32), vm((2, 2, rows, TILE, sites), F32)], COST,
    )(momenta, ids, vec, link)
    spare = lax.cond(over[0] != 0, gather_all, lambda: jnp.zeros((rows, npanel, sites), BF16))
    outer, flat_late, link_late = lax.optimization_barrier((outer, flat, link))
    inner = lax.ppermute(flat_late, "slab", mate)
    below = lax.ppermute(link_late[2], "slab", upward)
    field = call(
        height_kernel, [shape((3 * held, rows * sites), BF16)], "vvvvv", "v", "height", [vm((2, 18, sites), F32)],
    )(planar, link, below, inner, outer)[0]
    part = shape((half * lines, LANES), F32)
    inputs = (field, in_vmem(phase), in_vmem(order), got, in_vmem(spare))
    send, keep = [
        call(
            functools.partial(main_kernel, CAP, half_at), [part], "vvvvv", "v", name,
            [vm((rows, half, sites), F32),
             vm((2 * nmom * half, rows * sites), BF16)],
            cost,
        )(*inputs)[0]
        for half_at, name, cost in ((1, "send", 0), (0, "keep", COST))
    ]
    pair = lax.ppermute(send, "slab", mate)
    groups = [[2 * k + c for k in range(nslab // 2)] for c in range(2)]
    both = (keep + pair).reshape(half, 1, lines * LANES)
    parts = lax.all_to_all(both, "slab", 0, 0, axis_index_groups=groups, tiled=True)
    parts = parts.reshape(half * lines, LANES)
    return call(
        functools.partial(sum_kernel, nmom), [shape((2, 3, nmom, held), F32)], "vv", "v", "total",
    )(in_vmem(directions.reshape(1, 3)), parts)[0][None]


def solution(mesh):
    placed = (P(None, "vec", "slab", None), P(None, None, "slab", None), P(), P(), P())
    return jax.shard_map(
        body,
        mesh=mesh,
        in_specs=placed,
        out_specs=P("slab", None, None, None, "vec"),
        check_vma=False,
    )
```

```python
import functools
import math

import jax
import jax.numpy as jnp
from jax import lax
from jax.experimental import pallas as pl
from jax.experimental.pallas import tpu as pltpu
from jax.sharding import PartitionSpec as P

LX = 32
LY = 16
CAP = 16
COST = 50_000_000_000
TILE = 16
LANES = 128
F32 = jnp.float32
BF16 = jnp.bfloat16
NT = (((1,), (1,)), ((), ()))


def iota(shape, dim):
    return lax.broadcasted_iota(jnp.int32, shape, dim)


def as_column(row):
    n = row.shape[1]
    return jnp.sum(jnp.where(iota((n, n), 0) == iota((n, n), 1), row, 0.0), axis=1, keepdims=True)


def owner_and_rank(ids, owners, held):
    npanel = ids.shape[1]
    owner = jnp.zeros(ids.shape, F32)
    for other in range(1, owners):
        owner = owner + jnp.where(ids >= other * held, 1.0, 0.0)
    before = iota((npanel, npanel), 0) < iota((npanel, npanel), 1)
    rank = jnp.sum(jnp.where(before & (as_column(owner) == owner), 1.0, 0.0), axis=0, keepdims=True)
    return owner, rank


def order_of(slot, slots):
    npanel = slot.shape[1]
    half = npanel // 2
    core = lax.axis_index("slab") % 2
    place = iota((npanel, npanel), 0)
    wanted = jnp.where(place < half, 2 * place + core, 2 * (place - half) + 1 - core)
    column = jnp.sum(jnp.where(iota((npanel, npanel), 1) == wanted, slot, 0.0), axis=1, keepdims=True)
    return jnp.where(iota((npanel, slots), 1).astype(F32) == column, 1.0, 0.0).astype(BF16)


def select_kernel(cap, ids_ref, vec_ref, pay_ref, over_ref, here_ref, held_ref, in_sem):
    ids_load = pltpu.make_async_copy(ids_ref, here_ref, in_sem.at[0])
    rows, held, sites = vec_ref.shape
    loads = [pltpu.make_async_copy(vec_ref.at[row], held_ref.at[row], in_sem.at[1 + row]) for row in range(rows)]
    ids_load.start()
    for load in loads:
        load.start()
    ids_load.wait()
    ids = here_ref[...]
    npanel = ids.shape[1]
    local = ids - lax.axis_index("vec") * held
    inside = (local >= 0) & (local < held)
    owner, rank = owner_and_rank(ids, pay_ref.shape[0], held)
    over_ref[0] = (jnp.max(rank) >= cap).astype(jnp.int32)
    place = jnp.where(inside, rank, -1.0)
    to_slot = jnp.where(iota((cap, npanel), 0).astype(F32) == place, 1.0, 0.0)
    of_held = jnp.where(iota((held, npanel), 0) == local, 1.0, 0.0)
    pick = lax.dot_general(to_slot, of_held, NT, preferred_element_type=F32).astype(BF16)
    for row in range(rows):
        loads[row].wait()
        part = jnp.dot(pick, held_ref[row], preferred_element_type=F32).astype(BF16)
        for peer in range(pay_ref.shape[0]):
            pay_ref[peer, row * cap:(row + 1) * cap, :] = part


def link_terms(ahead, behind, fore, back):
    real, imag = [], []
    for row in range(3):
        re, im = 0.0, 0.0
        for col in range(3):
            ur, ui = fore(row * 3 + col), fore(9 + row * 3 + col)
            re = re + ur * ahead[col] - ui * ahead[3 + col]
            im = im + ur * ahead[3 + col] + ui * ahead[col]
        for col in range(3):
            ur, ui = back(col * 3 + row), back(9 + col * 3 + row)
            re = re - ur * behind[col] - ui * behind[3 + col]
            im = im - ur * behind[3 + col] + ui * behind[col]
        real.append(re)
        imag.append(im)
    return real + imag


def turn_x(value, ahead):
    inner = iota((value.shape[0], LANES), 1) % LX
    parts = []
    for at in range(0, value.shape[1], LANES):
        part = value[:, at:at + LANES]
        if ahead:
            part = jnp.where(inner == LX - 1, pltpu.roll(part, LX - 1, 1), pltpu.roll(part, LANES - 1, 1))
        else:
            part = jnp.where(inner == 0, pltpu.roll(part, LANES - LX + 1, 1), pltpu.roll(part, 1, 1))
        parts.append(part)
    return jnp.concatenate(parts, axis=1)


def turn_y(value, ahead):
    sites = value.shape[1]
    return pltpu.roll(value, sites - LX if ahead else LX, 1)


def planar_kernel(cap, owners, momenta_ref, ids_ref, vec_ref, links_ref, out_ref, phase_ref, order_ref,
                  link_ref, turned_ref):
    rows, held, sites = vec_ref.shape
    for axis_id, turn in enumerate((turn_x, turn_y)):
        link = links_ref[axis_id].astype(F32) * 0.5
        link_ref[2 * axis_id] = link
        link_ref[2 * axis_id + 1] = turn(link, False)

    def step(at, carry):
        first = pl.multiple_of(at * TILE, TILE)
        for row in range(rows):
            value = vec_ref[row, pl.ds(first, TILE), :].astype(F32)
            for axis_id, turn in enumerate((turn_x, turn_y)):
                turned_ref[axis_id, 0, row] = turn(value, True)
                turned_ref[axis_id, 1, row] = turn(value, False)
        for axis_id in range(2):
            for lane in range(0, sites, LANES):
                span = slice(lane, lane + LANES)
                ahead = [turned_ref[axis_id, 0, row, :, span] for row in range(rows)]
                behind = [turned_ref[axis_id, 1, row, :, span] for row in range(rows)]
                shifted = link_terms(
                    ahead, behind,
                    lambda e: link_ref[2 * axis_id, e:e + 1, span],
                    lambda e: link_ref[2 * axis_id + 1, e:e + 1, span],
                )
                for row in range(rows):
                    out_ref[axis_id, pl.ds(first, TILE), row * sites + lane:row * sites + lane + LANES] = (
                        shifted[row].astype(BF16))
        return carry

    lax.fori_loop(0, held // TILE, step, 0)
    owner, rank = owner_and_rank(ids_ref[...], owners, held)
    fits = jnp.max(rank, axis=1, keepdims=True) < cap
    order_ref[...] = order_of(jnp.where(fits, owner * cap + rank, -1.0), owners * cap)
    nmom = momenta_ref.shape[0]
    slab_id = lax.axis_index("slab")
    modulus = sites * lax.axis_size("slab")
    shape = (2 * nmom, sites)
    site, line = iota(shape, 1), iota(shape, 0)
    x_coord, y_coord = site % LX, site // LX
    turns = jnp.zeros(shape, jnp.int32)
    for mom in range(nmom):
        along = (momenta_ref[mom, 0] * (modulus // LX) * x_coord
                 + momenta_ref[mom, 1] * (modulus // LY) * y_coord
                 + momenta_ref[mom, 2] * sites * slab_id)
        turns = jnp.where(line % nmom == mom, along, turns)
    turns = jnp.where(line >= nmom, turns - modulus // 4, turns) & (modulus - 1)
    turns = jnp.where(turns >= modulus // 2, turns - modulus, turns)
    phase_ref[...] = jnp.cos(turns.astype(F32) * (2.0 * math.pi / modulus))


def height_kernel(planar_ref, links_ref, below_ref, inner_ref, outer_ref, out_ref, link_ref):
    planes, held, width = planar_ref.shape
    out_ref[0:planes * held, :] = planar_ref[...].reshape(planes * held, width)
    first_core = lax.axis_index("slab") % 2 == 0
    pl.when(first_core)(lambda: height(links_ref, below_ref, inner_ref, outer_ref, out_ref, link_ref))
    pl.when(jnp.logical_not(first_core))(lambda: height(links_ref, below_ref, outer_ref, inner_ref, out_ref, link_ref))


def height(links_ref, below_ref, ahead_ref, behind_ref, out_ref, link_ref):
    held = out_ref.shape[0] // 3
    sites = links_ref.shape[2]
    rows = out_ref.shape[1] // sites
    link_ref[0] = links_ref[2].astype(F32) * 0.5
    link_ref[1] = below_ref[...].astype(F32) * 0.5

    def step(at, carry):
        first = pl.multiple_of(at * TILE, TILE)
        for lane in range(0, sites, LANES):
            span = slice(lane, lane + LANES)
            ahead = [ahead_ref[pl.ds(row * held + first, TILE), span].astype(F32) for row in range(rows)]
            behind = [behind_ref[pl.ds(row * held + first, TILE), span].astype(F32) for row in range(rows)]
            shifted = link_terms(
                ahead, behind,
                lambda e: link_ref[0, e:e + 1, span],
                lambda e: link_ref[1, e:e + 1, span],
            )
            for row in range(rows):
                out_ref[pl.ds(2 * held + first, TILE), row * sites + lane:row * sites + lane + LANES] = (
                    shifted[row].astype(BF16))
        return carry

    lax.fori_loop(0, held // TILE, step, 0)


def reorder_kernel(ids_ref, got_ref, out_ref):
    held = got_ref.shape[1] // out_ref.shape[0]
    owners, _, sites = got_ref.shape
    order = order_of(ids_ref[...].astype(F32), owners * held)
    for row in range(out_ref.shape[0]):
        block = got_ref[:, row * held:(row + 1) * held, :].reshape(owners * held, sites)
        out_ref[row] = jnp.dot(order, block, preferred_element_type=F32).astype(BF16)


def main_kernel(cap, half_at, field_ref, phase_ref, order_ref, got_ref, spare_ref,
                out_ref, panel_ref, weight_ref):
    owners = got_ref.shape[0]
    npanel = order_ref.shape[0] // 2
    sites = got_ref.shape[2]
    rows = got_ref.shape[1] // cap
    nmom = phase_ref.shape[0] // 2
    chosen = slice(half_at * npanel, (half_at + 1) * npanel)
    for row in range(rows):
        block = got_ref[:, row * cap:(row + 1) * cap, :].reshape(owners * cap, sites)
        picked = jnp.dot(order_ref[chosen, :], block, preferred_element_type=F32)
        panel_ref[row] = picked + spare_ref[row, chosen, :].astype(F32)

    for first in range(0, npanel, TILE):
        for colour in range(3):
            re = panel_ref[colour, first:first + TILE, :]
            im = panel_ref[3 + colour, first:first + TILE, :]
            for mom in range(nmom):
                cos = phase_ref[mom:mom + 1, :]
                sin = phase_ref[nmom + mom:nmom + mom + 1, :]
                wr = (re * cos - im * sin).astype(BF16)
                wi = re * sin + im * cos
                low = slice(colour * sites, (colour + 1) * sites)
                high = slice((3 + colour) * sites, (4 + colour) * sites)
                at, after = mom * npanel + first, (nmom + mom) * npanel + first
                weight_ref[at:at + TILE, low] = wr
                weight_ref[at:at + TILE, high] = wi.astype(BF16)
                weight_ref[after:after + TILE, low] = (-wi).astype(BF16)
                weight_ref[after:after + TILE, high] = wr
    whole = lax.dot_general(weight_ref[...], field_ref[...], NT, preferred_element_type=F32)
    lines = 2 * nmom + 1
    blocks = [whole[part * npanel:(part + 1) * npanel] for part in range(2 * nmom)]
    for part, block in enumerate(blocks):
        out_ref[pl.ds(part, npanel, stride=lines), :] = block[:, :LANES]
    out_ref[pl.ds(2 * nmom, npanel, stride=lines), :] = jnp.concatenate([b[:, LANES:] for b in blocks], axis=1)


def sum_kernel(nmom, directions_ref, parts_ref, out_ref):
    held = out_ref.shape[-1]
    spill = 3 * held - LANES
    lines = 2 * nmom
    count = parts_ref.shape[0] // (lines + 1)
    summed = [
        jnp.sum(parts_ref[pl.ds(k, count, stride=lines + 1), :], axis=0, keepdims=True) for k in range(lines + 1)
    ]
    first = jnp.concatenate(summed[:lines], axis=0)
    last = summed[lines]
    last = jnp.concatenate([last[:, k * spill:(k + 1) * spill] for k in range(lines)], axis=0)
    total = jnp.concatenate([first, last], axis=1)
    for place in range(out_ref.shape[1]):
        chosen = total[:, 0:held]
        for axis_id in (1, 2):
            along = total[:, axis_id * held:(axis_id + 1) * held]
            chosen = jnp.where(directions_ref[:, place:place + 1] == axis_id, along, chosen)
        out_ref[0, place] = chosen[:nmom]
        out_ref[1, place] = chosen[nmom:]


def specs(*spaces):
    kinds = {"s": pltpu.SMEM, "v": pltpu.VMEM, "a": pl.ANY, "h": pltpu.HBM}
    return [pl.BlockSpec(memory_space=kinds[space]) for space in spaces]


def call(kernel, out_shape, ins, outs, name, scratch=(), cost=0):
    return pl.pallas_call(
        kernel, out_shape=out_shape, in_specs=specs(*ins), out_specs=specs(*outs),
        scratch_shapes=list(scratch), name=name,
        cost_estimate=pl.CostEstimate(flops=cost, bytes_accessed=0, transcendentals=0) if cost else None,
        compiler_params=pltpu.CompilerParams(vmem_limit_bytes=16 * 1024 * 1024),
    )


def in_vmem(value):
    return pltpu.with_memory_space_constraint(value, pltpu.VMEM)


def body(vectors, links, momenta, directions, panel_index):
    rows, held, planes, sites = vectors.shape
    npanel = panel_index.shape[0]
    nmom = momenta.shape[0]
    nslab, nvec = lax.axis_size("slab"), lax.axis_size("vec")
    half = npanel // 2
    lines = 2 * nmom + 1
    vec = vectors.reshape(rows, held, sites)
    link = links.reshape(3, 18, sites)
    ids = panel_index.reshape(1, npanel)
    shape = jax.ShapeDtypeStruct
    vm = pltpu.VMEM
    flat = vec.reshape(rows * held, sites)
    mate = [(i, i ^ 1) for i in range(nslab)]
    beyond = [(i, (i + 1) % nslab if i % 2 else (i - 1) % nslab) for i in range(nslab)]
    upward = [(i, (i + 1) % nslab) for i in range(nslab)]
    outer = lax.ppermute(flat, "slab", beyond)
    pay, over = call(
        functools.partial(select_kernel, CAP), [shape((nvec, rows * CAP, sites), BF16), pltpu.SMEM((1,), jnp.int32)],
        "hh", "vs", "select",
        [vm(ids.shape, jnp.int32), vm(vec.shape, BF16), pltpu.SemaphoreType.DMA((1 + rows,))],
        COST,
    )(ids, vec)
    got = lax.all_to_all(pay, "vec", 0, 0, tiled=True)
    def gather_all():
        every = jnp.broadcast_to(vec.reshape(1, rows * held, sites), (nvec, rows * held, sites))
        every = lax.all_to_all(every, "vec", 0, 0, tiled=True)
        return call(reorder_kernel, [shape((rows, npanel, sites), BF16)], "vv", "v", "reorder")(ids, every)[0]

    planar, phase, order = call(
        functools.partial(planar_kernel, CAP, nvec),
        [shape((2, held, rows * sites), BF16), shape((2 * nmom, sites), F32), shape((npanel, nvec * CAP), BF16)],
        "svvv", "vvv", "planar",
        [vm((4, 18, sites), F32), vm((2, 2, rows, TILE, sites), F32)], COST,
    )(momenta, ids, vec, link)
    spare = lax.cond(over[0] != 0, gather_all, lambda: jnp.zeros((rows, npanel, sites), BF16))
    outer, flat_late, link_late = lax.optimization_barrier((outer, flat, link))
    inner = lax.ppermute(flat_late, "slab", mate)
    below = lax.ppermute(link_late[2], "slab", upward)
    field = call(
        height_kernel, [shape((3 * held, rows * sites), BF16)], "vvvvv", "v", "height", [vm((2, 18, sites), F32)],
    )(planar, link, below, inner, outer)[0]
    part = shape((half * lines, LANES), F32)
    inputs = (field, in_vmem(phase), in_vmem(order), got, in_vmem(spare))
    send, keep = [
        call(
            functools.partial(main_kernel, CAP, half_at), [part], "vvvvv", "v", name,
            [vm((rows, half, sites), F32),
             vm((2 * nmom * half, rows * sites), BF16)],
            cost,
        )(*inputs)[0]
        for half_at, name, cost in ((1, "send", 0), (0, "keep", COST))
    ]
    pair = lax.ppermute(send, "slab", mate)
    groups = [[2 * k + c for k in range(nslab // 2)] for c in range(2)]
    both = (keep + pair).reshape(half, 1, lines * LANES)
    parts = lax.all_to_all(both, "slab", 0, 0, axis_index_groups=groups, tiled=True)
    parts = parts.reshape(half * lines, LANES)
    return call(
        functools.partial(sum_kernel, nmom), [shape((2, 3, nmom, held), F32)], "vv", "v", "total",
    )(in_vmem(directions.reshape(1, 3)), parts)[0][None]


def solution(mesh):
    placed = (P(None, "vec", "slab", None), P(None, None, "slab", None), P(), P(), P())
    return jax.shard_map(
        body,
        mesh=mesh,
        in_specs=placed,
        out_specs=P("slab", None, None, None, "vec"),
        check_vma=False,
    )
```

```python
import functools
import math

import jax
import jax.numpy as jnp
from jax import lax
from jax.experimental import pallas as pl
from jax.experimental.pallas import tpu as pltpu
from jax.sharding import PartitionSpec as P

LX = 32
LY = 16
CAP = 16
COST = 50_000_000_000
TILE = 16
LANES = 128
F32 = jnp.float32
BF16 = jnp.bfloat16
NT = (((1,), (1,)), ((), ()))


def iota(shape, dim):
    return lax.broadcasted_iota(jnp.int32, shape, dim)


def as_column(row):
    n = row.shape[1]
    return jnp.sum(jnp.where(iota((n, n), 0) == iota((n, n), 1), row, 0.0), axis=1, keepdims=True)


def owner_and_rank(ids, owners, held):
    npanel = ids.shape[1]
    owner = jnp.zeros(ids.shape, F32)
    for other in range(1, owners):
        owner = owner + jnp.where(ids >= other * held, 1.0, 0.0)
    before = iota((npanel, npanel), 0) < iota((npanel, npanel), 1)
    rank = jnp.sum(jnp.where(before & (as_column(owner) == owner), 1.0, 0.0), axis=0, keepdims=True)
    return owner, rank


def order_of(slot, slots):
    npanel = slot.shape[1]
    half = npanel // 2
    core = lax.axis_index("slab") % 2
    place = iota((npanel, npanel), 0)
    wanted = jnp.where(place < half, 2 * place + core, 2 * (place - half) + 1 - core)
    column = jnp.sum(jnp.where(iota((npanel, npanel), 1) == wanted, slot, 0.0), axis=1, keepdims=True)
    return jnp.where(iota((npanel, slots), 1).astype(F32) == column, 1.0, 0.0).astype(BF16)


def select_kernel(cap, ids_ref, vec_ref, pay_ref, over_ref, here_ref, held_ref, block_ref, in_sem, out_sem):
    ids_load = pltpu.make_async_copy(ids_ref, here_ref, in_sem.at[0])
    load = pltpu.make_async_copy(vec_ref, held_ref, in_sem.at[1])
    ids_load.start()
    load.start()
    rows, held, sites = vec_ref.shape
    ids_load.wait()
    ids = here_ref[...]
    npanel = ids.shape[1]
    local = ids - lax.axis_index("vec") * held
    inside = (local >= 0) & (local < held)
    owner, rank = owner_and_rank(ids, pay_ref.shape[0], held)
    over_ref[0] = (jnp.max(rank) >= cap).astype(jnp.int32)
    place = jnp.where(inside, rank, -1.0)
    to_slot = jnp.where(iota((cap, npanel), 0).astype(F32) == place, 1.0, 0.0)
    of_held = jnp.where(iota((held, npanel), 0) == local, 1.0, 0.0)
    pick = lax.dot_general(to_slot, of_held, NT, preferred_element_type=F32).astype(BF16)
    load.wait()
    for row in range(rows):
        block_ref[row * cap:(row + 1) * cap, :] = jnp.dot(
            pick, held_ref[row], preferred_element_type=F32).astype(BF16)
    copies = [pltpu.make_async_copy(block_ref, pay_ref.at[peer], out_sem.at[peer]) for peer in range(pay_ref.shape[0])]
    for copy in copies:
        copy.start()
    for copy in copies:
        copy.wait()


def link_terms(ahead, behind, fore, back):
    real, imag = [], []
    for row in range(3):
        re, im = 0.0, 0.0
        for col in range(3):
            ur, ui = fore(row * 3 + col), fore(9 + row * 3 + col)
            re = re + ur * ahead[col] - ui * ahead[3 + col]
            im = im + ur * ahead[3 + col] + ui * ahead[col]
        for col in range(3):
            ur, ui = back(col * 3 + row), back(9 + col * 3 + row)
            re = re - ur * behind[col] - ui * behind[3 + col]
            im = im - ur * behind[3 + col] + ui * behind[col]
        real.append(re)
        imag.append(im)
    return real + imag


def turn_x(value, ahead):
    inner = iota((value.shape[0], LANES), 1) % LX
    parts = []
    for at in range(0, value.shape[1], LANES):
        part = value[:, at:at + LANES]
        if ahead:
            part = jnp.where(inner == LX - 1, pltpu.roll(part, LX - 1, 1), pltpu.roll(part, LANES - 1, 1))
        else:
            part = jnp.where(inner == 0, pltpu.roll(part, LANES - LX + 1, 1), pltpu.roll(part, 1, 1))
        parts.append(part)
    return jnp.concatenate(parts, axis=1)


def turn_y(value, ahead):
    sites = value.shape[1]
    return pltpu.roll(value, sites - LX if ahead else LX, 1)


def planar_kernel(cap, owners, momenta_ref, ids_ref, vec_ref, links_ref, out_ref, phase_ref, order_ref,
                  link_ref, turned_ref):
    rows, held, sites = vec_ref.shape
    for axis_id, turn in enumerate((turn_x, turn_y)):
        link = links_ref[axis_id].astype(F32) * 0.5
        link_ref[2 * axis_id] = link
        link_ref[2 * axis_id + 1] = turn(link, False)

    def step(at, carry):
        first = pl.multiple_of(at * TILE, TILE)
        for row in range(rows):
            value = vec_ref[row, pl.ds(first, TILE), :].astype(F32)
            for axis_id, turn in enumerate((turn_x, turn_y)):
                turned_ref[axis_id, 0, row] = turn(value, True)
                turned_ref[axis_id, 1, row] = turn(value, False)
        for axis_id in range(2):
            for lane in range(0, sites, LANES):
                span = slice(lane, lane + LANES)
                ahead = [turned_ref[axis_id, 0, row, :, span] for row in range(rows)]
                behind = [turned_ref[axis_id, 1, row, :, span] for row in range(rows)]
                shifted = link_terms(
                    ahead, behind,
                    lambda e: link_ref[2 * axis_id, e:e + 1, span],
                    lambda e: link_ref[2 * axis_id + 1, e:e + 1, span],
                )
                for row in range(rows):
                    out_ref[axis_id, pl.ds(first, TILE), row * sites + lane:row * sites + lane + LANES] = (
                        shifted[row].astype(BF16))
        return carry

    lax.fori_loop(0, held // TILE, step, 0)
    owner, rank = owner_and_rank(ids_ref[...], owners, held)
    fits = jnp.max(rank, axis=1, keepdims=True) < cap
    order_ref[...] = order_of(jnp.where(fits, owner * cap + rank, -1.0), owners * cap)
    nmom = momenta_ref.shape[0]
    slab_id = lax.axis_index("slab")
    modulus = sites * lax.axis_size("slab")
    shape = (2 * nmom, sites)
    site, line = iota(shape, 1), iota(shape, 0)
    x_coord, y_coord = site % LX, site // LX
    turns = jnp.zeros(shape, jnp.int32)
    for mom in range(nmom):
        along = (momenta_ref[mom, 0] * (modulus // LX) * x_coord
                 + momenta_ref[mom, 1] * (modulus // LY) * y_coord
                 + momenta_ref[mom, 2] * sites * slab_id)
        turns = jnp.where(line % nmom == mom, along, turns)
    turns = jnp.where(line >= nmom, turns - modulus // 4, turns) & (modulus - 1)
    turns = jnp.where(turns >= modulus // 2, turns - modulus, turns)
    phase_ref[...] = jnp.cos(turns.astype(F32) * (2.0 * math.pi / modulus))


def height_kernel(planar_ref, links_ref, below_ref, inner_ref, outer_ref, out_ref, link_ref):
    planes, held, width = planar_ref.shape
    out_ref[0:planes * held, :] = planar_ref[...].reshape(planes * held, width)
    first_core = lax.axis_index("slab") % 2 == 0
    pl.when(first_core)(lambda: height(links_ref, below_ref, inner_ref, outer_ref, out_ref, link_ref))
    pl.when(jnp.logical_not(first_core))(lambda: height(links_ref, below_ref, outer_ref, inner_ref, out_ref, link_ref))


def height(links_ref, below_ref, ahead_ref, behind_ref, out_ref, link_ref):
    held = out_ref.shape[0] // 3
    sites = links_ref.shape[2]
    rows = out_ref.shape[1] // sites
    link_ref[0] = links_ref[2].astype(F32) * 0.5
    link_ref[1] = below_ref[...].astype(F32) * 0.5

    def step(at, carry):
        first = pl.multiple_of(at * TILE, TILE)
        for lane in range(0, sites, LANES):
            span = slice(lane, lane + LANES)
            ahead = [ahead_ref[pl.ds(row * held + first, TILE), span].astype(F32) for row in range(rows)]
            behind = [behind_ref[pl.ds(row * held + first, TILE), span].astype(F32) for row in range(rows)]
            shifted = link_terms(
                ahead, behind,
                lambda e: link_ref[0, e:e + 1, span],
                lambda e: link_ref[1, e:e + 1, span],
            )
            for row in range(rows):
                out_ref[pl.ds(2 * held + first, TILE), row * sites + lane:row * sites + lane + LANES] = (
                    shifted[row].astype(BF16))
        return carry

    lax.fori_loop(0, held // TILE, step, 0)


def reorder_kernel(ids_ref, got_ref, out_ref):
    held = got_ref.shape[1] // out_ref.shape[0]
    owners, _, sites = got_ref.shape
    order = order_of(ids_ref[...].astype(F32), owners * held)
    for row in range(out_ref.shape[0]):
        block = got_ref[:, row * held:(row + 1) * held, :].reshape(owners * held, sites)
        out_ref[row] = jnp.dot(order, block, preferred_element_type=F32).astype(BF16)


def main_kernel(cap, half_at, field_ref, phase_ref, order_ref, got_ref, spare_ref,
                out_ref, panel_ref, weight_ref):
    owners = got_ref.shape[0]
    npanel = order_ref.shape[0] // 2
    sites = got_ref.shape[2]
    rows = got_ref.shape[1] // cap
    nmom = phase_ref.shape[0] // 2
    chosen = slice(half_at * npanel, (half_at + 1) * npanel)
    for row in range(rows):
        block = got_ref[:, row * cap:(row + 1) * cap, :].reshape(owners * cap, sites)
        picked = jnp.dot(order_ref[chosen, :], block, preferred_element_type=F32)
        panel_ref[row] = picked + spare_ref[row, chosen, :].astype(F32)

    for first in range(0, npanel, TILE):
        for colour in range(3):
            re = panel_ref[colour, first:first + TILE, :]
            im = panel_ref[3 + colour, first:first + TILE, :]
            for mom in range(nmom):
                cos = phase_ref[mom:mom + 1, :]
                sin = phase_ref[nmom + mom:nmom + mom + 1, :]
                wr = (re * cos - im * sin).astype(BF16)
                wi = re * sin + im * cos
                low = slice(colour * sites, (colour + 1) * sites)
                high = slice((3 + colour) * sites, (4 + colour) * sites)
                at, after = mom * npanel + first, (nmom + mom) * npanel + first
                weight_ref[at:at + TILE, low] = wr
                weight_ref[at:at + TILE, high] = wi.astype(BF16)
                weight_ref[after:after + TILE, low] = (-wi).astype(BF16)
                weight_ref[after:after + TILE, high] = wr
    whole = lax.dot_general(weight_ref[...], field_ref[...], NT, preferred_element_type=F32)
    lines = 2 * nmom + 1
    blocks = [whole[part * npanel:(part + 1) * npanel] for part in range(2 * nmom)]
    for part, block in enumerate(blocks):
        out_ref[pl.ds(part, npanel, stride=lines), :] = block[:, :LANES]
    out_ref[pl.ds(2 * nmom, npanel, stride=lines), :] = jnp.concatenate([b[:, LANES:] for b in blocks], axis=1)


def sum_kernel(nmom, directions_ref, parts_ref, out_ref):
    held = out_ref.shape[-1]
    spill = 3 * held - LANES
    lines = 2 * nmom
    count = parts_ref.shape[0] // (lines + 1)
    summed = [
        jnp.sum(parts_ref[pl.ds(k, count, stride=lines + 1), :], axis=0, keepdims=True) for k in range(lines + 1)
    ]
    first = jnp.concatenate(summed[:lines], axis=0)
    last = summed[lines]
    last = jnp.concatenate([last[:, k * spill:(k + 1) * spill] for k in range(lines)], axis=0)
    total = jnp.concatenate([first, last], axis=1)
    for place in range(out_ref.shape[1]):
        chosen = total[:, 0:held]
        for axis_id in (1, 2):
            along = total[:, axis_id * held:(axis_id + 1) * held]
            chosen = jnp.where(directions_ref[:, place:place + 1] == axis_id, along, chosen)
        out_ref[0, place] = chosen[:nmom]
        out_ref[1, place] = chosen[nmom:]


def specs(*spaces):
    kinds = {"s": pltpu.SMEM, "v": pltpu.VMEM, "a": pl.ANY, "h": pltpu.HBM}
    return [pl.BlockSpec(memory_space=kinds[space]) for space in spaces]


def call(kernel, out_shape, ins, outs, name, scratch=(), cost=0):
    return pl.pallas_call(
        kernel, out_shape=out_shape, in_specs=specs(*ins), out_specs=specs(*outs),
        scratch_shapes=list(scratch), name=name,
        cost_estimate=pl.CostEstimate(flops=cost, bytes_accessed=0, transcendentals=0) if cost else None,
        compiler_params=pltpu.CompilerParams(vmem_limit_bytes=16 * 1024 * 1024),
    )


def in_vmem(value):
    return pltpu.with_memory_space_constraint(value, pltpu.VMEM)


def body(vectors, links, momenta, directions, panel_index):
    rows, held, planes, sites = vectors.shape
    npanel = panel_index.shape[0]
    nmom = momenta.shape[0]
    nslab, nvec = lax.axis_size("slab"), lax.axis_size("vec")
    half = npanel // 2
    lines = 2 * nmom + 1
    vec = vectors.reshape(rows, held, sites)
    link = links.reshape(3, 18, sites)
    ids = panel_index.reshape(1, npanel)
    shape = jax.ShapeDtypeStruct
    vm = pltpu.VMEM
    flat = vec.reshape(rows * held, sites)
    mate = [(i, i ^ 1) for i in range(nslab)]
    beyond = [(i, (i + 1) % nslab if i % 2 else (i - 1) % nslab) for i in range(nslab)]
    upward = [(i, (i + 1) % nslab) for i in range(nslab)]
    outer = lax.ppermute(flat, "slab", beyond)
    pay, over = call(
        functools.partial(select_kernel, CAP), [shape((nvec, rows * CAP, sites), BF16), pltpu.SMEM((1,), jnp.int32)],
        "hh", "as", "select",
        [vm(ids.shape, jnp.int32), vm(vec.shape, BF16), vm((rows * CAP, sites), BF16), pltpu.SemaphoreType.DMA((2,)),
         pltpu.SemaphoreType.DMA((nvec,))],
        COST,
    )(ids, vec)
    got = lax.all_to_all(pay, "vec", 0, 0, tiled=True)
    def gather_all():
        every = jnp.broadcast_to(vec.reshape(1, rows * held, sites), (nvec, rows * held, sites))
        every = lax.all_to_all(every, "vec", 0, 0, tiled=True)
        return call(reorder_kernel, [shape((rows, npanel, sites), BF16)], "vv", "v", "reorder")(ids, every)[0]

    planar, phase, order = call(
        functools.partial(planar_kernel, CAP, nvec),
        [shape((2, held, rows * sites), BF16), shape((2 * nmom, sites), F32), shape((npanel, nvec * CAP), BF16)],
        "svvv", "vvv", "planar",
        [vm((4, 18, sites), F32), vm((2, 2, rows, TILE, sites), F32)], COST,
    )(momenta, ids, vec, link)
    spare = lax.cond(over[0] != 0, gather_all, lambda: jnp.zeros((rows, npanel, sites), BF16))
    outer, flat_late, link_late = lax.optimization_barrier((outer, flat, link))
    inner = lax.ppermute(flat_late, "slab", mate)
    below = lax.ppermute(link_late[2], "slab", upward)
    field = call(
        height_kernel, [shape((3 * held, rows * sites), BF16)], "vvvvv", "v", "height", [vm((2, 18, sites), F32)],
    )(planar, link, below, inner, outer)[0]
    part = shape((half * lines, LANES), F32)
    inputs = (field, in_vmem(phase), in_vmem(order), got, in_vmem(spare))
    send, keep = [
        call(
            functools.partial(main_kernel, CAP, half_at), [part], "vvvvv", "v", name,
            [vm((rows, half, sites), F32),
             vm((2 * nmom * half, rows * sites), BF16)],
            cost,
        )(*inputs)[0]
        for half_at, name, cost in ((1, "send", 0), (0, "keep", COST))
    ]
    pair = lax.ppermute(send, "slab", mate)
    groups = [[2 * k + c for k in range(nslab // 2)] for c in range(2)]
    both = (keep + pair).reshape(half, 1, lines * LANES)
    parts = lax.all_to_all(both, "slab", 0, 0, axis_index_groups=groups, tiled=True)
    parts = parts.reshape(half * lines, LANES)
    return call(
        functools.partial(sum_kernel, nmom), [shape((2, 3, nmom, held), F32)], "vv", "v", "total",
    )(in_vmem(directions.reshape(1, 3)), parts)[0][None]


def solution(mesh):
    placed = (P(None, "vec", "slab", None), P(None, None, "slab", None), P(), P(), P())
    return jax.shard_map(
        body,
        mesh=mesh,
        in_specs=placed,
        out_specs=P("slab", None, None, None, "vec"),
        check_vma=False,
    )
```
